256 devices in a mesh: view: 32 (over z, y), mp: 8 (over x, core).
Axes of the slice: x: 4, y: 4, z: 8, core: 2. Of those that a mesh axis runs over, the one named last changes fastest.
Arguments:
- tokens: bfloat16 [128, 384, 1024], P('view', None, 'mp'), may hold values from -6 to 6
- pairs: int32 [512, 2], P('view'), may hold values from 0 to 127, as said below
- w_embed: bfloat16 [1024, 768], replicated, may hold values from -0.1875 to 0.1875
- w_query: bfloat16 [2, 768, 768], replicated, may hold values from -8 to 8
- w_keyval: bfloat16 [2, 768, 1536], replicated, may hold values from -0.21875 to 0.21875
- w_out: bfloat16 [2, 768, 768], replicated, may hold values from -0.21875 to 0.21875
- w_head: bfloat16 [2, 4, 768], replicated, may hold values from -0.21875 to 0.21875
- gains: float32 [2, 3, 768], replicated, may hold values from 0.1 to 1.9
Outputs:
- view_sums: float32 [128, 4, 384], P('view')
The draws below stay inside these ranges and needn't reach their ends.
Inputs may be any that keep to these rules, and one draw needn't show every extreme that they name: Owner of a view: view // 4. Among the 32 sides of the pairs of one index of view, at most 2 name views of one owner, and in every such block some owner is named exactly 2 times. The two views of a pair differ.
All inputs are finite; a program needn't handle non-finite values.
Results may differ from the reference program's by a relative error of at most 0.012.
Values may be sent and summed in bfloat16 or wider, within the bound.
A program may use at most 128 MiB of HBM per device.

```python
import jax
import jax.numpy as jnp
from jax import lax

E = 1024
D = 768
HEADS = 12
TOKV = 384
VIEW_DEV = 4
PAIR_DEV = 2
CAP = 2
VIEWS = 128
PAIRS = 512
N_VIEW = 32
N_MP = 8


def draw_pairs(key, part):
    block_pairs = PAIR_DEV * N_MP
    block_sides = 2 * block_pairs
    listed = N_VIEW * CAP

    def one_block(block_key):
        keys = jax.random.split(block_key, 6)
        owner_of = jnp.arange(listed, dtype=jnp.int32) // CAP
        chosen = jax.random.randint(keys[0], (), 0, N_VIEW)
        ranks = jax.random.permutation(keys[1], listed).astype(jnp.int32)
        scores = jnp.where(owner_of == chosen, -1 - jnp.arange(listed, dtype=jnp.int32), ranks)
        order = jnp.argsort(scores, stable=True)
        picked = jnp.take(owner_of, order)[:block_sides]
        picked = jax.random.permutation(keys[2], picked)
        owners = picked.reshape(block_pairs, 2)
        first = jax.random.randint(keys[3], (block_pairs,), 0, VIEW_DEV)
        offset = jax.random.randint(keys[4], (block_pairs,), 1, VIEW_DEV)
        loose = jax.random.randint(keys[5], (block_pairs,), 0, VIEW_DEV)
        second = jnp.where(owners[:, 0] == owners[:, 1], (first + offset) % VIEW_DEV, loose)
        return jnp.stack([owners[:, 0] * VIEW_DEV + first, owners[:, 1] * VIEW_DEV + second], axis=1)
    blocks = jax.vmap(one_block)(jax.random.split(key, N_VIEW))
    return blocks.reshape(PAIRS, 2).astype(jnp.int32)


def draw_w_query(key, part):
    base = jax.random.normal(key, (2, D, D), jnp.float32) * D ** (-0.5)
    return jnp.clip(base, -8.0, 8.0).astype(jnp.bfloat16)


def block_levels(key, extent, pieces, least, top_value):
    gain, own = 1.0, jax.random.fold_in(key, 6)
    for dim, parts in pieces:
        steps = jnp.exp(jax.random.uniform(jax.random.fold_in(own, dim), (parts,), jnp.float32, least / len(pieces), top_value / len(pieces)))
        gain = gain * jnp.repeat(steps, extent[dim] // parts).reshape([-1 if axis == dim else 1 for axis in range(len(extent))])
    return gain


def gaussian(stream_key, shape, scale, limit, pieces=(), held_as=jnp.bfloat16):
    result = scale * jax.random.normal(stream_key, shape, jnp.float32)
    if pieces:
        result = result * block_levels(stream_key, shape, pieces, -0.22, 0.18)
    return jnp.clip(result, -limit, limit).astype(held_as)


def setup_inputs(seed: int = 0) -> dict:
    streams_of = jax.random.split(jax.random.key(seed), 9)
    return {
        "tokens": gaussian(streams_of[0], (VIEWS, TOKV, E), 1.0, 6.0, ((0, 32), (2, 8))),
        "pairs": draw_pairs(jax.random.fold_in(streams_of[8], 71), 0),
        "w_embed": gaussian(streams_of[2], (E, D), E ** -0.5, 0.1875),
        "w_query": draw_w_query(jax.random.fold_in(streams_of[8], 71), 0),
        "w_keyval": gaussian(streams_of[4], (2, D, 2 * D), D ** -0.5, 0.21875),
        "w_out": gaussian(streams_of[5], (2, D, D), D ** -0.5, 0.21875),
        "w_head": gaussian(streams_of[6], (2, 4, D), D ** -0.5, 0.21875),
        "gains": jnp.clip(1.0 + 0.18 * jax.random.normal(streams_of[7], (2, 3, D), jnp.float32), 0.1, 1.9),
    }


def layer_norm(values):
    mean = lax.optimization_barrier(jnp.mean(values, axis=-1, keepdims=True))
    centred = values - mean
    var = lax.optimization_barrier(jnp.mean(centred * centred, axis=-1, keepdims=True))
    return centred * lax.rsqrt(var + 1e-06)

def decode_pair(emb, w_query, w_keyval, w_out, w_head, gains):
    width = emb.shape[-1]
    head_size = width // HEADS
    records = []
    for side in range(2):
        other = 1 - side
        query_in = (layer_norm(emb[side].astype(jnp.float32)) * gains[side, 0]).astype(jnp.bfloat16)
        memory_in = (layer_norm(emb[other].astype(jnp.float32)) * gains[side, 1]).astype(jnp.bfloat16)
        query = jnp.dot(query_in, w_query[side], preferred_element_type=jnp.float32).astype(jnp.bfloat16)
        keyval = jnp.dot(memory_in, w_keyval[side], preferred_element_type=jnp.float32).astype(jnp.bfloat16)
        count = query.shape[0]
        query_h = query.reshape(count, HEADS, head_size).astype(jnp.float32)
        key_h = keyval[:, :width].reshape(count, HEADS, head_size).astype(jnp.float32)
        value_h = keyval[:, width:].reshape(count, HEADS, head_size).astype(jnp.float32)
        scores = jnp.einsum('qhd,khd->hqk', query_h, key_h) * (1.0 / head_size ** 0.5)
        weights = jax.nn.softmax(scores, axis=-1)
        probs = weights.astype(jnp.bfloat16).astype(jnp.float32)
        context = jnp.einsum('hqk,khd->qhd', probs, value_h).astype(jnp.bfloat16).reshape(count, width)
        updated = emb[side].astype(jnp.float32) + jnp.dot(context, w_out[side], preferred_element_type=jnp.float32)
        final = (layer_norm(updated) * gains[side, 2]).astype(jnp.bfloat16)
        head = jnp.dot(w_head[side], final.T, preferred_element_type=jnp.float32)
        conf = 1.0 + jnp.exp(head[3])
        records.append(jnp.concatenate([conf[None, :] * head[:3], conf[None, :]], axis=0))
    return jnp.stack(records, axis=0)

def reference(tokens, pairs, w_embed, w_query, w_keyval, w_out, w_head, gains):
    start = jnp.zeros((VIEWS, 4, TOKV), jnp.float32)

    def one_pair(total, pair):
        chosen = jnp.take(tokens, pair.astype(jnp.int32), axis=0)
        emb = jnp.dot(chosen.reshape(2 * TOKV, E), w_embed, preferred_element_type=jnp.float32)
        emb = emb.astype(jnp.bfloat16).reshape(2, TOKV, D)
        record = decode_pair(emb, w_query, w_keyval, w_out, w_head, gains)
        total = total.at[pair[0]].add(record[0])
        total = total.at[pair[1]].add(record[1])
        return (total, None)
    total, unused = lax.scan(one_pair, start, pairs)
    return total
```

```python
import jax
import jax.numpy as jnp
from jax import lax
from jax.experimental import pallas as pl
from jax.experimental.pallas import tpu as pltpu
from jax.sharding import PartitionSpec as P

HEADS = 12


def layer_norm(values):
    mean = jnp.mean(values, axis=-1, keepdims=True)
    centred = values - mean
    var = jnp.mean(centred * centred, axis=-1, keepdims=True)
    return centred * lax.rsqrt(var + 1e-06)


def decode_sides(emb, w_query, w_keyval, w_out, w_head, gains):
    width = emb.shape[-1]
    head_size = width // HEADS
    count = emb.shape[0]
    tokv = emb.shape[2]
    records = []
    for side in range(2):
        other = 1 - side
        query_in = (layer_norm(emb[:, side].astype(jnp.float32)) * gains[side, 0]).astype(
            jnp.bfloat16
        )
        memory_in = (layer_norm(emb[:, other].astype(jnp.float32)) * gains[side, 1]).astype(
            jnp.bfloat16
        )
        query = jnp.einsum(
            "ptd,de->pte", query_in, w_query[side], preferred_element_type=jnp.float32
        ).astype(jnp.bfloat16)
        keyval = jnp.einsum(
            "ptd,de->pte", memory_in, w_keyval[side], preferred_element_type=jnp.float32
        ).astype(jnp.bfloat16)
        query_h = query.reshape(count, tokv, HEADS, head_size)
        key_h = keyval[..., :width].reshape(count, tokv, HEADS, head_size)
        value_h = keyval[..., width:].reshape(count, tokv, HEADS, head_size)
        scores = jnp.einsum(
            "pqhd,pkhd->phqk", query_h, key_h, preferred_element_type=jnp.float32
        ) * (1.0 / head_size**0.5)
        probs = jax.nn.softmax(scores, axis=-1).astype(jnp.bfloat16)
        context = jnp.einsum("phqk,pkhd->pqhd", probs, value_h, preferred_element_type=jnp.float32)
        context = context.astype(jnp.bfloat16).reshape(count, tokv, width)
        updated = emb[:, side].astype(jnp.float32) + jnp.einsum(
            "ptd,de->pte", context, w_out[side], preferred_element_type=jnp.float32
        )
        final = (layer_norm(updated) * gains[side, 2]).astype(jnp.bfloat16)
        head = jnp.einsum("cd,ptd->pct", w_head[side], final, preferred_element_type=jnp.float32)
        conf = 1.0 + jnp.exp(head[:, 3])
        records.append(jnp.concatenate([conf[:, None, :] * head[:, :3], conf[:, None, :]], axis=1))
    return jnp.stack(records, axis=1)


def copy_block(index_ref, source_ref, target_ref):
    target_ref[...] = source_ref[...]


def pick_sides(every, side_views):
    count = side_views.shape[0]
    part, width = every.shape[1:]
    return pl.pallas_call(
        copy_block,
        out_shape=jax.ShapeDtypeStruct((count, part, width), every.dtype),
        grid_spec=pltpu.PrefetchScalarGridSpec(
            num_scalar_prefetch=1,
            grid=(count,),
            in_specs=[pl.BlockSpec((1, part, width), lambda i, index: (index[i], 0, 0))],
            out_specs=pl.BlockSpec((1, part, width), lambda i, index: (i, 0, 0)),
        ),
    )(side_views, every)


def on_device(tokens, pairs, w_embed, w_query, w_keyval, w_out, w_head, gains):
    view_count = lax.axis_size("view")
    column_count = lax.axis_size("mp")
    me = lax.axis_index("view")
    view_dev, tokv, feat_shard = tokens.shape
    width = w_embed.shape[1]
    block_pairs = pairs.shape[0]
    pair_dev = block_pairs // column_count
    side_count = 2 * block_pairs
    cap = max(2, (side_count + view_count - 1) // view_count)
    part = tokv // column_count
    all_pairs = lax.all_gather(pairs, "view", axis=0, tiled=True)
    full = lax.all_to_all(tokens, "mp", split_axis=1, concat_axis=2, tiled=True)
    emb = jnp.dot(
        full.reshape(view_dev * part, feat_shard * column_count),
        w_embed,
        preferred_element_type=jnp.float32,
    ).astype(jnp.bfloat16).reshape(view_dev, part, width)
    every = lax.all_gather(emb, "view", axis=0, tiled=True)
    side_views = pairs.reshape(side_count)
    chosen = pick_sides(every, side_views)
    parcel = chosen.reshape(column_count, pair_dev * 2, part, width)
    arrived = lax.all_to_all(parcel, "mp", split_axis=0, concat_axis=0, tiled=False)
    sides = jnp.transpose(arrived, (1, 0, 2, 3)).reshape(pair_dev, 2, tokv, width)
    results = decode_sides(sides, w_query, w_keyval, w_out, w_head, gains)

    chunk = 4 * tokv // column_count
    shares = results.reshape(2 * pair_dev, column_count, chunk)
    shares = lax.all_to_all(shares, "mp", split_axis=1, concat_axis=0, tiled=False)
    shares = shares.reshape(side_count, chunk)
    owners = side_views // view_dev
    positions = jnp.arange(side_count, dtype=jnp.int32)
    earlier = jnp.logical_and(
        owners[:, None] == owners[None, :], positions[None, :] < positions[:, None]
    )
    slot_index = owners * cap + jnp.sum(earlier, axis=1)
    match = jnp.arange(view_count * cap, dtype=jnp.int32)[:, None] == slot_index[None, :]
    outgoing = jnp.sum(jnp.where(match[..., None], shares[None], 0.0), axis=1).reshape(view_count, cap, chunk)
    incoming = lax.all_to_all(outgoing, "view", split_axis=0, concat_axis=0, tiled=True)

    asked = all_pairs.reshape(view_count, side_count)
    mine = asked // view_dev == me
    rank = jnp.sum(
        jnp.logical_and(mine[:, None, :], positions[None, None, :] < positions[None, :, None]), axis=2
    )
    slot = jnp.arange(cap, dtype=jnp.int32)
    hit = jnp.logical_and(mine[:, None, :], rank[:, None, :] == slot[None, :, None])
    local = jnp.sum(jnp.where(hit, (asked % view_dev + 1)[:, None, :], 0), axis=2) - 1
    picks = local[None] == jnp.arange(view_dev, dtype=jnp.int32)[:, None, None]
    owned = jnp.sum(jnp.where(picks[..., None], incoming[None], 0.0), axis=(1, 2))
    gathered = lax.all_gather(owned, "mp", axis=1, tiled=True)
    return gathered.reshape(view_dev, 4, tokv)


def solution(mesh):
    return jax.shard_map(
        on_device,
        mesh=mesh,
        in_specs=(P("view", None, "mp"), P("view", None), P(), P(), P(), P(), P(), P()),
        out_specs=P("view", None, None),
        check_vma=False,
    )
```

```python
import functools

import jax
import jax.numpy as jnp
from jax import lax
from jax.experimental import pallas as pl
from jax.experimental.pallas import tpu as pltpu
from jax.sharding import PartitionSpec as P

HEADS = 12


def layer_norm(values):
    mean = jnp.mean(values, axis=-1, keepdims=True)
    centred = values - mean
    var = jnp.mean(centred * centred, axis=-1, keepdims=True)
    return centred * lax.rsqrt(var + 1e-06)


def decode_sides(emb, w_query, w_keyval, w_out, w_head, gains):
    width = emb.shape[-1]
    head_size = width // HEADS
    count = emb.shape[0]
    tokv = emb.shape[2]
    records = []
    for side in range(2):
        other = 1 - side
        query_in = (layer_norm(emb[:, side].astype(jnp.float32)) * gains[side, 0]).astype(
            jnp.bfloat16
        )
        memory_in = (layer_norm(emb[:, other].astype(jnp.float32)) * gains[side, 1]).astype(
            jnp.bfloat16
        )
        query = jnp.einsum(
            "ptd,de->pte", query_in, w_query[side], preferred_element_type=jnp.float32
        ).astype(jnp.bfloat16)
        keyval = jnp.einsum(
            "ptd,de->pte", memory_in, w_keyval[side], preferred_element_type=jnp.float32
        ).astype(jnp.bfloat16)
        query_h = query.reshape(count, tokv, HEADS, head_size)
        key_h = keyval[..., :width].reshape(count, tokv, HEADS, head_size)
        value_h = keyval[..., width:].reshape(count, tokv, HEADS, head_size)
        scores = jnp.einsum(
            "pqhd,pkhd->phqk", query_h, key_h, preferred_element_type=jnp.float32
        ) * (1.0 / head_size**0.5)
        probs = jax.nn.softmax(scores, axis=-1).astype(jnp.bfloat16)
        context = jnp.einsum("phqk,pkhd->pqhd", probs, value_h, preferred_element_type=jnp.float32)
        context = context.astype(jnp.bfloat16).reshape(count, tokv, width)
        updated = emb[:, side].astype(jnp.float32) + jnp.einsum(
            "ptd,de->pte", context, w_out[side], preferred_element_type=jnp.float32
        )
        final = (layer_norm(updated) * gains[side, 2]).astype(jnp.bfloat16)
        head = jnp.einsum("cd,ptd->pct", w_head[side], final, preferred_element_type=jnp.float32)
        conf = 1.0 + jnp.exp(head[:, 3])
        records.append(jnp.concatenate([conf[:, None, :] * head[:, :3], conf[:, None, :]], axis=1))
    return jnp.stack(records, axis=1)


NY = 4
ROWS = 16
MESH = pl.DeviceIdType.MESH


def remote(source, target, send, arrive, device):
    return pltpu.make_async_remote_copy(
        src_ref=source,
        dst_ref=target,
        send_sem=send,
        recv_sem=arrive,
        device_id=device,
        device_id_type=MESH,
    )


def gather_kernel(nz, nm, chunks, tokens, wanted, places, w_embed, out, full, w_near, w_held, slots, parcels, *rest):
    pools = rest[:chunks]
    rest = rest[chunks:]
    held = [rest[c * nz : (c + 1) * nz] for c in range(chunks)]
    rest = rest[chunks * nz :]
    (t_send, t_recv, w_send, w_recv, z_send, z_recv, y_send, y_recv, f_send, f_recv, x_send, x_recv, local) = rest
    view = lax.axis_index("view")
    me = lax.axis_index("mp")
    z = view // NY
    y = view % NY
    part = tokens.shape[1] // nm
    feat = tokens.shape[2]
    view_dev = tokens.shape[0]
    sides = places.shape[0] // nm

    def at_z(step):
        return (lax.rem(z + step + nz, nz) * NY + y, me)

    def at_y(step):
        return (z * NY + lax.rem(y + step + NY, NY), me)

    def at_m(step):
        return (view, lax.rem(me + step, nm))

    barrier = pltpu.get_barrier_semaphore()
    peers = [at_m(o) for o in range(1, nm)] + [at_z(1), at_z(-1)] + [at_y(o) for o in range(1, NY)]
    for peer in peers:
        pl.semaphore_signal(barrier, inc=1, device_id=peer, device_id_type=MESH)
    pl.semaphore_wait(barrier, len(peers))

    sent = []

    def start(copy):
        copy.start()
        sent.append(copy)
        return copy

    arriving = []
    for o in range(1, nm):
        j = lax.rem(me + o, nm)
        arriving.append(
            start(
                remote(
                    tokens.at[:, pl.ds(pl.multiple_of(j * part, ROWS), part), :],
                    full.at[:, :, pl.ds(pl.multiple_of(me * feat, 128), feat)],
                    t_send.at[o],
                    t_recv.at[o],
                    at_m(o),
                )
            )
        )
    own = pltpu.make_async_copy(
        tokens.at[:, pl.ds(pl.multiple_of(me * part, ROWS), part), :],
        full.at[:, :, pl.ds(pl.multiple_of(me * feat, 128), feat)],
        local.at[0],
    )
    own.start()
    asking = [
        start(remote(wanted, w_near.at[NY - o], w_send.at[o], w_recv.at[NY - o], at_y(o)))
        for o in range(1, NY)
    ]
    own_wanted = pltpu.make_async_copy(wanted, w_near.at[0], local.at[1])
    own_wanted.start()
    own_wanted.wait()
    for copy in asking:
        copy.wait_recv()
    to_scalars = pltpu.make_async_copy(w_near, w_held, local.at[2])
    to_scalars.start()
    to_scalars.wait()
    own.wait()
    for copy in arriving:
        copy.wait_recv()
    for c in range(chunks):
        rows = full[:, c * ROWS : (c + 1) * ROWS, :].reshape(view_dev * ROWS, nm * feat)
        emb = jnp.dot(rows, w_embed[...], preferred_element_type=jnp.float32)
        held[c][0][...] = emb.astype(jnp.bfloat16).reshape(view_dev, ROWS, -1)

    up = [nz // 2 if c % 2 == 0 else (nz - 1) // 2 for c in range(chunks)]
    down = [nz - 1 - u for u in up]
    steps = max(nz // 2, 1) + 1
    lag = 2
    z_copy, y_copy, f_copy, x_copy = {}, {}, {}, {}

    def z_forward(c, d, way):
        target = (d - way) % nz
        z_copy[c, target] = start(
            remote(
                held[c][d],
                held[c][target],
                z_send.at[c, target],
                z_recv.at[c, target],
                at_z(way),
            )
        )

    def chosen(c, d, dy, r):
        owner = lax.rem(z + d, nz) * NY + y
        return held[c][d][w_held[dy, 0, owner * 2 + r]]

    def y_start(c, d):
        slots[c, 0, d, 0] = chosen(c, d, 1, 0)
        slots[c, 0, d, 1] = chosen(c, d, 1, 1)
        slots[c, 0, d, 2] = chosen(c, d, 2, 0)
        y_copy[c, 0, d] = start(
            remote(
                slots.at[c, 0, d],
                pools[c].at[pl.ds(3 * d, 3)],
                y_send.at[c, 0, d],
                y_recv.at[c, 0, d],
                at_y(1),
            )
        )
        slots[c, 1, d, 0] = chosen(c, d, 3, 0)
        slots[c, 1, d, 1] = chosen(c, d, 3, 1)
        slots[c, 1, d, 2] = chosen(c, d, 2, 1)
        y_copy[c, 1, d] = start(
            remote(
                slots.at[c, 1, d],
                pools[c].at[pl.ds(3 * nz + 3 * d, 3)],
                y_send.at[c, 1, d],
                y_recv.at[c, 1, d],
                at_y(-1),
            )
        )
        pools[c][8 * nz + 2 * d] = chosen(c, d, 0, 0)
        pools[c][8 * nz + 2 * d + 1] = chosen(c, d, 0, 1)

    def y_forward(c, d):
        for way in range(2):
            y_copy[c, way, d].wait_recv()
            f_copy[c, way, d] = start(
                remote(
                    pools[c].at[pl.ds(3 * nz * way + 3 * d + 2, 1)],
                    pools[c].at[pl.ds(6 * nz + nz * way + d, 1)],
                    f_send.at[c, way, d],
                    f_recv.at[c, way, d],
                    at_y(1 - 2 * way),
                )
            )

    def offsets(c, t):
        found = [0] if t == 0 else []
        if 1 <= t <= up[c]:
            found.append(nz - t)
        if 1 <= t <= down[c]:
            found.append(t)
        return found

    def x_start(c):
        for d in range(nz):
            for way in range(2):
                f_copy[c, way, d].wait_recv()
        for k in range(nm * sides):
            parcels[c, k] = pools[c][places[k]]
        for o in range(1, nm):
            j = lax.rem(me + o, nm)
            x_copy[c, o] = start(
                remote(
                    parcels.at[c, pl.ds(j * sides, sides)],
                    out.at[:, pl.ds(pl.multiple_of(me * part + c * ROWS, ROWS), ROWS), :],
                    x_send.at[c, o],
                    x_recv.at[c, o],
                    at_m(o),
                )
            )
        x_copy[c, 0] = pltpu.make_async_copy(
            parcels.at[c, pl.ds(me * sides, sides)],
            out.at[:, pl.ds(pl.multiple_of(me * part + c * ROWS, ROWS), ROWS), :],
            local.at[3 + c],
        )
        x_copy[c, 0].start()

    order = [(c, t) for c in range(chunks) for t in range(steps)]
    for i in range(len(order) + 2 * lag):
        if i < len(order):
            c, t = order[i]
            for d in offsets(c, t):
                if d:
                    z_copy[c, d].wait_recv()
                if t < up[c] and (t == 0 or d == nz - t):
                    z_forward(c, d, 1)
                if t < down[c] and (t == 0 or d == t):
                    z_forward(c, d, -1)
            for d in offsets(c, t):
                y_start(c, d)
        if 0 <= i - lag < len(order):
            c, t = order[i - lag]
            for d in offsets(c, t):
                y_forward(c, d)
        if 0 <= i - 2 * lag < len(order):
            c, t = order[i - 2 * lag]
            if t == steps - 1:
                x_start(c)
    for c in range(chunks):
        x_copy[c, 0].wait()
        for o in range(1, nm):
            x_copy[c, o].wait_recv()
    for copy in sent:
        copy.wait_send()


def gather_sides(tokens, wanted, places, w_embed):
    nz = lax.axis_size("view") // NY
    nm = lax.axis_size("mp")
    view_dev, tokv, feat = tokens.shape
    width = w_embed.shape[1]
    part = tokv // nm
    chunks = part // ROWS
    count = places.shape[0]
    block = (ROWS, width)
    vmem = pl.BlockSpec(memory_space=pltpu.VMEM)
    dma = pltpu.SemaphoreType.DMA
    return pl.pallas_call(
        functools.partial(gather_kernel, nz, nm, chunks),
        out_shape=jax.ShapeDtypeStruct((count // nm, tokv, width), jnp.bfloat16),
        in_specs=[vmem, vmem, pl.BlockSpec(memory_space=pltpu.SMEM), vmem],
        out_specs=vmem,
        scratch_shapes=[
            pltpu.VMEM((view_dev, part, nm * feat), jnp.bfloat16),
            pltpu.VMEM((NY,) + wanted.shape, jnp.int32),
            pltpu.SMEM((NY,) + wanted.shape, jnp.int32),
            pltpu.VMEM((chunks, 2, nz, 3) + block, jnp.bfloat16),
            pltpu.VMEM((chunks, count) + block, jnp.bfloat16),
        ]
        + [pltpu.VMEM((10 * nz,) + block, jnp.bfloat16)] * chunks
        + [pltpu.VMEM((view_dev,) + block, jnp.bfloat16)] * (chunks * nz)
        + [dma((nm,))] * 2
        + [dma((NY,))] * 2
        + [dma((chunks, nz))] * 2
        + [dma((chunks, 2, nz))] * 4
        + [dma((chunks, nm))] * 2
        + [dma((3 + chunks,))],
        compiler_params=pltpu.CompilerParams(
            collective_id=0, has_side_effects=True, vmem_limit_bytes=48 * 2**20
        ),
    )(tokens, wanted, places, w_embed)


def plan_sides(side_views, view_dev, cap):
    view_count = lax.axis_size("view")
    nz = view_count // NY
    me = lax.axis_index("view")
    count = side_views.shape[0]
    owners = side_views // view_dev
    positions = jnp.arange(count, dtype=jnp.int32)
    earlier = jnp.logical_and(
        owners[:, None] == owners[None, :], positions[None, :] < positions[:, None]
    )
    rank = jnp.sum(earlier, axis=1)
    slot_index = owners * cap + rank
    match = jnp.arange(128, dtype=jnp.int32)[:, None] == slot_index[None, :]
    wanted = jnp.sum(jnp.where(match, (side_views % view_dev)[None, :], 0), axis=1)
    wanted = jnp.broadcast_to(wanted[None, :], (8, 128))
    d = (owners // NY - me // NY + nz) % nz
    rel = (owners % NY - me % NY + NY) % NY
    places = jnp.where(
        rel == 0,
        8 * nz + 2 * d + rank,
        jnp.where(
            rel == 3,
            3 * d + rank,
            jnp.where(rel == 1, 3 * nz + 3 * d + rank, 6 * nz + nz * rank + d),
        ),
    )
    return wanted, places


def on_device(tokens, pairs, w_embed, w_query, w_keyval, w_out, w_head, gains):
    view_count = lax.axis_size("view")
    column_count = lax.axis_size("mp")
    me = lax.axis_index("view")
    view_dev, tokv, unused = tokens.shape
    block_pairs = pairs.shape[0]
    pair_dev = block_pairs // column_count
    side_count = 2 * block_pairs
    cap = max(2, (side_count + view_count - 1) // view_count)
    all_pairs = lax.all_gather(pairs, "view", axis=0, tiled=True)
    side_views = pairs.reshape(side_count)
    wanted, places = plan_sides(side_views, view_dev, cap)
    sides = gather_sides(tokens, wanted, places, w_embed).reshape(pair_dev, 2, tokv, -1)
    results = decode_sides(sides, w_query, w_keyval, w_out, w_head, gains)

    chunk = 4 * tokv // column_count
    shares = results.reshape(2 * pair_dev, column_count, chunk)
    shares = lax.all_to_all(shares, "mp", split_axis=1, concat_axis=0, tiled=False)
    shares = shares.reshape(side_count, chunk)
    owners = side_views // view_dev
    positions = jnp.arange(side_count, dtype=jnp.int32)
    earlier = jnp.logical_and(
        owners[:, None] == owners[None, :], positions[None, :] < positions[:, None]
    )
    slot_index = owners * cap + jnp.sum(earlier, axis=1)
    match = jnp.arange(view_count * cap, dtype=jnp.int32)[:, None] == slot_index[None, :]
    outgoing = jnp.sum(jnp.where(match[..., None], shares[None], 0.0), axis=1).reshape(view_count, cap, chunk)
    incoming = lax.all_to_all(outgoing, "view", split_axis=0, concat_axis=0, tiled=True)

    asked = all_pairs.reshape(view_count, side_count)
    mine = asked // view_dev == me
    rank = jnp.sum(
        jnp.logical_and(mine[:, None, :], positions[None, None, :] < positions[None, :, None]), axis=2
    )
    slot = jnp.arange(cap, dtype=jnp.int32)
    hit = jnp.logical_and(mine[:, None, :], rank[:, None, :] == slot[None, :, None])
    local = jnp.sum(jnp.where(hit, (asked % view_dev + 1)[:, None, :], 0), axis=2) - 1
    picks = local[None] == jnp.arange(view_dev, dtype=jnp.int32)[:, None, None]
    owned = jnp.sum(jnp.where(picks[..., None], incoming[None], 0.0), axis=(1, 2))
    gathered = lax.all_gather(owned, "mp", axis=1, tiled=True)
    return gathered.reshape(view_dev, 4, tokv)


def solution(mesh):
    return jax.shard_map(
        on_device,
        mesh=mesh,
        in_specs=(P("view", None, "mp"), P("view", None), P(), P(), P(), P(), P(), P()),
        out_specs=P("view", None, None),
        check_vma=False,
    )
```

```python
import functools

import jax
import jax.numpy as jnp
from jax import lax
from jax.experimental import pallas as pl
from jax.experimental.pallas import tpu as pltpu
from jax.sharding import PartitionSpec as P

HEADS = 12


NY = 4
ROWS = 16
MESH = pl.DeviceIdType.MESH


def remote(source, target, send, arrive, device):
    return pltpu.make_async_remote_copy(
        src_ref=source,
        dst_ref=target,
        send_sem=send,
        recv_sem=arrive,
        device_id=device,
        device_id_type=MESH,
    )


def gather_kernel(nz, nm, chunks, tokens, wanted, places, w_embed, out, full, w_near, w_held, slots, parcels, *rest):
    pools = rest[:chunks]
    rest = rest[chunks:]
    held = [rest[c * nz : (c + 1) * nz] for c in range(chunks)]
    rest = rest[chunks * nz :]
    (t_send, t_recv, w_send, w_recv, z_send, z_recv, y_send, y_recv, f_send, f_recv, x_send, x_recv, local) = rest
    view = lax.axis_index("view")
    me = lax.axis_index("mp")
    z = view // NY
    y = view % NY
    part = tokens.shape[1] // nm
    feat = tokens.shape[2]
    view_dev = tokens.shape[0]
    sides = places.shape[0] // nm

    def at_z(step):
        return (lax.rem(z + step + nz, nz) * NY + y, me)

    def at_y(step):
        return (z * NY + lax.rem(y + step + NY, NY), me)

    def at_m(step):
        return (view, lax.rem(me + step, nm))

    barrier = pltpu.get_barrier_semaphore()
    peers = [at_m(o) for o in range(1, nm)] + [at_z(1), at_z(-1)] + [at_y(o) for o in range(1, NY)]
    for peer in peers:
        pl.semaphore_signal(barrier, inc=1, device_id=peer, device_id_type=MESH)
    pl.semaphore_wait(barrier, len(peers))

    sent = []

    def start(copy):
        copy.start()
        sent.append(copy)
        return copy

    arriving = []
    for o in range(1, nm):
        j = lax.rem(me + o, nm)
        arriving.append(
            start(
                remote(
                    tokens.at[:, pl.ds(pl.multiple_of(j * part, ROWS), part), :],
                    full.at[:, :, pl.ds(pl.multiple_of(me * feat, 128), feat)],
                    t_send.at[o],
                    t_recv.at[o],
                    at_m(o),
                )
            )
        )
    own = pltpu.make_async_copy(
        tokens.at[:, pl.ds(pl.multiple_of(me * part, ROWS), part), :],
        full.at[:, :, pl.ds(pl.multiple_of(me * feat, 128), feat)],
        local.at[0],
    )
    own.start()
    asking = [
        start(remote(wanted, w_near.at[NY - o], w_send.at[o], w_recv.at[NY - o], at_y(o)))
        for o in range(1, NY)
    ]
    own_wanted = pltpu.make_async_copy(wanted, w_near.at[0], local.at[1])
    own_wanted.start()
    own_wanted.wait()
    for copy in asking:
        copy.wait_recv()
    to_scalars = pltpu.make_async_copy(w_near, w_held, local.at[2])
    to_scalars.start()
    to_scalars.wait()
    own.wait()
    for copy in arriving:
        copy.wait_recv()
    for c in range(chunks):
        rows = full[:, c * ROWS : (c + 1) * ROWS, :].reshape(view_dev * ROWS, nm * feat)
        emb = jnp.dot(rows, w_embed[...], preferred_element_type=jnp.float32)
        held[c][0][...] = emb.astype(jnp.bfloat16).reshape(view_dev, ROWS, -1)

    up = [nz // 2 if c % 2 == 0 else (nz - 1) // 2 for c in range(chunks)]
    down = [nz - 1 - u for u in up]
    steps = max(nz // 2, 1) + 1
    lag = 2
    z_copy, y_copy, f_copy, x_copy = {}, {}, {}, {}

    def z_forward(c, d, way):
        target = (d - way) % nz
        z_copy[c, target] = start(
            remote(
                held[c][d],
                held[c][target],
                z_send.at[c, target],
                z_recv.at[c, target],
                at_z(way),
            )
        )

    def chosen(c, d, dy, r):
        owner = lax.rem(z + d, nz) * NY + y
        return held[c][d][w_held[dy, 0, owner * 2 + r]]

    def y_start(c, d):
        slots[c, 0, d, 0] = chosen(c, d, 1, 0)
        slots[c, 0, d, 1] = chosen(c, d, 1, 1)
        slots[c, 0, d, 2] = chosen(c, d, 2, 0)
        y_copy[c, 0, d] = start(
            remote(
                slots.at[c, 0, d],
                pools[c].at[pl.ds(3 * d, 3)],
                y_send.at[c, 0, d],
                y_recv.at[c, 0, d],
                at_y(1),
            )
        )
        slots[c, 1, d, 0] = chosen(c, d, 3, 0)
        slots[c, 1, d, 1] = chosen(c, d, 3, 1)
        slots[c, 1, d, 2] = chosen(c, d, 2, 1)
        y_copy[c, 1, d] = start(
            remote(
                slots.at[c, 1, d],
                pools[c].at[pl.ds(3 * nz + 3 * d, 3)],
                y_send.at[c, 1, d],
                y_recv.at[c, 1, d],
                at_y(-1),
            )
        )
        pools[c][8 * nz + 2 * d] = chosen(c, d, 0, 0)
        pools[c][8 * nz + 2 * d + 1] = chosen(c, d, 0, 1)

    def y_forward(c, d):
        for way in range(2):
            y_copy[c, way, d].wait_recv()
            f_copy[c, way, d] = start(
                remote(
                    pools[c].at[pl.ds(3 * nz * way + 3 * d + 2, 1)],
                    pools[c].at[pl.ds(6 * nz + nz * way + d, 1)],
                    f_send.at[c, way, d],
                    f_recv.at[c, way, d],
                    at_y(1 - 2 * way),
                )
            )

    def offsets(c, t):
        found = [0] if t == 0 else []
        if 1 <= t <= up[c]:
            found.append(nz - t)
        if 1 <= t <= down[c]:
            found.append(t)
        return found

    def x_start(c):
        for d in range(nz):
            for way in range(2):
                f_copy[c, way, d].wait_recv()
        for k in range(nm * sides):
            parcels[c, k] = pools[c][places[k]]
        for o in range(1, nm):
            j = lax.rem(me + o, nm)
            x_copy[c, o] = start(
                remote(
                    parcels.at[c, pl.ds(j * sides, sides)],
                    out.at[:, pl.ds(pl.multiple_of(me * part + c * ROWS, ROWS), ROWS), :],
                    x_send.at[c, o],
                    x_recv.at[c, o],
                    at_m(o),
                )
            )
        x_copy[c, 0] = pltpu.make_async_copy(
            parcels.at[c, pl.ds(me * sides, sides)],
            out.at[:, pl.ds(pl.multiple_of(me * part + c * ROWS, ROWS), ROWS), :],
            local.at[3 + c],
        )
        x_copy[c, 0].start()

    order = [(c, t) for c in range(chunks) for t in range(steps)]
    for i in range(len(order) + 2 * lag):
        if i < len(order):
            c, t = order[i]
            for d in offsets(c, t):
                if d:
                    z_copy[c, d].wait_recv()
                if t < up[c] and (t == 0 or d == nz - t):
                    z_forward(c, d, 1)
                if t < down[c] and (t == 0 or d == t):
                    z_forward(c, d, -1)
            for d in offsets(c, t):
                y_start(c, d)
        if 0 <= i - lag < len(order):
            c, t = order[i - lag]
            for d in offsets(c, t):
                y_forward(c, d)
        if 0 <= i - 2 * lag < len(order):
            c, t = order[i - 2 * lag]
            if t == steps - 1:
                x_start(c)
    for c in range(chunks):
        x_copy[c, 0].wait()
        for o in range(1, nm):
            x_copy[c, o].wait_recv()
    for copy in sent:
        copy.wait_send()


def gather_sides(tokens, wanted, places, w_embed):
    nz = lax.axis_size("view") // NY
    nm = lax.axis_size("mp")
    view_dev, tokv, feat = tokens.shape
    width = w_embed.shape[1]
    part = tokv // nm
    chunks = part // ROWS
    count = places.shape[0]
    block = (ROWS, width)
    vmem = pl.BlockSpec(memory_space=pltpu.VMEM)
    dma = pltpu.SemaphoreType.DMA
    return pl.pallas_call(
        functools.partial(gather_kernel, nz, nm, chunks),
        out_shape=jax.ShapeDtypeStruct((count // nm, tokv, width), jnp.bfloat16),
        in_specs=[vmem, vmem, pl.BlockSpec(memory_space=pltpu.SMEM), vmem],
        out_specs=vmem,
        scratch_shapes=[
            pltpu.VMEM((view_dev, part, nm * feat), jnp.bfloat16),
            pltpu.VMEM((NY,) + wanted.shape, jnp.int32),
            pltpu.SMEM((NY,) + wanted.shape, jnp.int32),
            pltpu.VMEM((chunks, 2, nz, 3) + block, jnp.bfloat16),
            pltpu.VMEM((chunks, count) + block, jnp.bfloat16),
        ]
        + [pltpu.VMEM((10 * nz,) + block, jnp.bfloat16)] * chunks
        + [pltpu.VMEM((view_dev,) + block, jnp.bfloat16)] * (chunks * nz)
        + [dma((nm,))] * 2
        + [dma((NY,))] * 2
        + [dma((chunks, nz))] * 2
        + [dma((chunks, 2, nz))] * 4
        + [dma((chunks, nm))] * 2
        + [dma((3 + chunks,))],
        compiler_params=pltpu.CompilerParams(
            collective_id=0, has_side_effects=True, vmem_limit_bytes=48 * 2**20
        ),
    )(tokens, wanted, places, w_embed)


def plan_sides(side_views, view_dev, cap):
    view_count = lax.axis_size("view")
    nz = view_count // NY
    me = lax.axis_index("view")
    count = side_views.shape[0]
    owners = side_views // view_dev
    positions = jnp.arange(count, dtype=jnp.int32)
    earlier = jnp.logical_and(
        owners[:, None] == owners[None, :], positions[None, :] < positions[:, None]
    )
    rank = jnp.sum(earlier, axis=1)
    slot_index = owners * cap + rank
    match = jnp.arange(128, dtype=jnp.int32)[:, None] == slot_index[None, :]
    wanted = jnp.sum(jnp.where(match, (side_views % view_dev)[None, :], 0), axis=1)
    wanted = jnp.broadcast_to(wanted[None, :], (8, 128))
    d = (owners // NY - me // NY + nz) % nz
    rel = (owners % NY - me % NY + NY) % NY
    places = jnp.where(
        rel == 0,
        8 * nz + 2 * d + rank,
        jnp.where(
            rel == 3,
            3 * d + rank,
            jnp.where(rel == 1, 3 * nz + 3 * d + rank, 6 * nz + nz * rank + d),
        ),
    )
    return wanted, places


def normal(values):
    mean = jnp.mean(values, axis=-1, keepdims=True)
    centred = values - mean
    var = jnp.mean(centred * centred, axis=-1, keepdims=True)
    return centred * lax.rsqrt(var + 1e-06)


def decode_kernel(sides, spread, w_query, w_keyval, w_out, w_head, gains, sums, query, keyval, context, out, block, toward, came, mine_sum, every, s1, r1, s2, r2, s3, r3):
    count, tokv, width = sides.shape
    nm, nv = out.shape[0], toward.shape[0]
    view = lax.axis_index("view")
    me = lax.axis_index("mp")
    barrier = pltpu.get_barrier_semaphore()
    columns_peers = [(view, lax.rem(me + o, nm)) for o in range(1, nm)]
    view_peers = [(lax.rem(view + o, nv), me) for o in range(1, nv)]
    for peer in columns_peers + view_peers:
        pl.semaphore_signal(barrier, inc=1, device_id=peer, device_id_type=MESH)
    size = width // HEADS
    scale = 1.4426950408889634 / size**0.5
    f32, bf16 = jnp.float32, jnp.bfloat16

    @pl.loop(0, count)
    def one_side(i):
        side = lax.rem(i, 2)
        gain = gains[side]
        query_in = (normal(sides[i].astype(f32)) * gain[0:1]).astype(bf16)
        query[...] = jnp.dot(query_in, w_query[side], preferred_element_type=f32).astype(bf16)
        memory_in = (normal(sides[i + 1 - 2 * side].astype(f32)) * gain[1:2]).astype(bf16)
        keyval[...] = jnp.dot(memory_in, w_keyval[side], preferred_element_type=f32).astype(bf16)
        lane = lax.broadcasted_iota(jnp.int32, (tokv, 2 * size), 1)
        first = lane < size
        ones = jnp.ones((tokv, 2 * size), bf16)
        for h in range(0, HEADS, 2):
            columns = slice(h * size, (h + 2) * size)
            both = query[:, columns]
            keys = keyval[:, columns]
            values = jnp.concatenate(
                [keyval[:, width + h * size : width + (h + 2) * size], ones], axis=1
            )
            found = []
            for half in range(2):
                mine = jnp.where(first if half == 0 else jnp.logical_not(first), both, jnp.zeros_like(both))
                scores = lax.dot_general(
                    mine, keys, (((1,), (1,)), ((), ())), preferred_element_type=f32
                )
                top = jnp.max(scores, axis=-1, keepdims=True)
                probs = jnp.exp2((scores - top) * scale).astype(bf16)
                total = jnp.dot(probs, values, preferred_element_type=f32)
                found.append(total[:, : 2 * size] / total[:, 2 * size :])
            context[:, columns] = jnp.where(first, found[0], found[1]).astype(bf16)
        updated = sides[i].astype(f32) + jnp.dot(
            context[...], w_out[side], preferred_element_type=f32
        )
        final = (normal(updated) * gain[2:3]).astype(bf16)
        head = lax.dot_general(
            w_head[side], final, (((1,), (1,)), ((), ())), preferred_element_type=f32
        )
        conf = 1.0 + jnp.exp(head[3:4])
        for c in range(4):
            record = conf * head[c : c + 1] if c < 3 else conf
            for b in range(tokv // 128):
                row = c * (tokv // 128) + b
                out[row // 2, pl.ds(row % 2 * count + i, 1), :] = record[:, b * 128 : (b + 1) * 128]

    pl.semaphore_wait(barrier, nm + nv - 2)
    sent, coming = [], []

    def start(copy):
        copy.start()
        sent.append(copy)
        coming.append(copy)

    def arrive():
        for copy in coming:
            copy.wait_recv()
        coming.clear()

    for o in range(1, nm):
        start(remote(out.at[lax.rem(me + o, nm)], block.at[me], s1.at[o], r1.at[o], columns_peers[o - 1]))
    block[me] = out[me]
    arrive()
    toward[...] = jnp.dot(
        spread[...],
        block[...].reshape(nm * 8, 128),
        precision=lax.Precision.HIGHEST,
        preferred_element_type=f32,
    ).reshape(nv, 8, 128)
    for o in range(1, nv):
        start(remote(toward.at[lax.rem(view + o, nv)], came.at[view], s2.at[o], r2.at[o], view_peers[o - 1]))
    came[view] = toward[view]
    arrive()
    mine_sum[...] = jnp.sum(came[...], axis=0)
    for o in range(1, nm):
        start(remote(mine_sum, every.at[me], s3.at[o], r3.at[o], columns_peers[o - 1]))
    every[me] = mine_sum[...]
    arrive()
    blocks = tokv // 128
    for local in range(sums.shape[0]):
        for row in range(4 * blocks):
            place = row % blocks * 128
            sums[local, row // blocks, place : place + 128] = every[row // 2, local * 2 + row % 2]
    for copy in sent:
        copy.wait_send()


def plan_spread(side_views, views, view_dev, nm):
    count = side_views.shape[0] // nm
    column = jnp.arange(nm * 2 * count, dtype=jnp.int32)
    row = jnp.arange(views * 2, dtype=jnp.int32)
    column_view = jnp.broadcast_to(side_views.reshape(nm, 1, count), (nm, 2, count)).reshape(-1)
    same = jnp.logical_and(
        row[:, None] // 2 == column_view[None, :], row[:, None] % 2 == (column // count % 2)[None, :]
    )
    return same.astype(jnp.float32)


def decode(sides, spread, w_query, w_keyval, w_out, w_head, gains):
    count, tokv, width = sides.shape
    nm = lax.axis_size("mp")
    nv = lax.axis_size("view")
    view_dev = spread.shape[0] // (2 * nv)
    vmem = pl.BlockSpec(memory_space=pltpu.VMEM)
    dma = pltpu.SemaphoreType.DMA
    f32 = jnp.float32
    pad = lambda a: jnp.pad(a, ((0, 0), (0, 8 - a.shape[1]), (0, 0)))
    return pl.pallas_call(
        decode_kernel,
        out_shape=jax.ShapeDtypeStruct((view_dev, 4, tokv), f32),
        in_specs=[vmem] * 7,
        out_specs=vmem,
        scratch_shapes=[
            pltpu.VMEM((tokv, width), jnp.bfloat16),
            pltpu.VMEM((tokv, 2 * width), jnp.bfloat16),
            pltpu.VMEM((tokv, width), jnp.bfloat16),
            pltpu.VMEM((nm, 8, 128), f32),
            pltpu.VMEM((nm, 8, 128), f32),
            pltpu.VMEM((nv, 8, 128), f32),
            pltpu.VMEM((nv, 8, 128), f32),
            pltpu.VMEM((8, 128), f32),
            pltpu.VMEM((nm, 8, 128), f32),
            dma((nm,)),
            dma((nm,)),
            dma((nv,)),
            dma((nv,)),
            dma((nm,)),
            dma((nm,)),
        ],
        compiler_params=pltpu.CompilerParams(
            collective_id=1, has_side_effects=True, vmem_limit_bytes=52 * 2**20
        ),
    )(sides, spread, w_query, w_keyval, w_out, pad(w_head), pad(gains))


def on_device(tokens, pairs, w_embed, w_query, w_keyval, w_out, w_head, gains):
    view_count = lax.axis_size("view")
    column_count = lax.axis_size("mp")
    view_dev = tokens.shape[0]
    side_count = 2 * pairs.shape[0]
    cap = max(2, (side_count + view_count - 1) // view_count)
    side_views = pairs.reshape(side_count)
    wanted, places = plan_sides(side_views, view_dev, cap)
    spread = plan_spread(side_views, view_count * view_dev, view_dev, column_count)
    sides = gather_sides(tokens, wanted, places, w_embed)
    return decode(sides, spread, w_query, w_keyval, w_out, w_head, gains)


def solution(mesh):
    return jax.shard_map(
        on_device,
        mesh=mesh,
        in_specs=(P("view", None, "mp"), P("view", None), P(), P(), P(), P(), P(), P()),
        out_specs=P("view", None, None),
        check_vma=False,
    )
```

```python
import functools

import jax
import jax.numpy as jnp
from jax import lax
from jax.experimental import pallas as pl
from jax.experimental.pallas import tpu as pltpu
from jax.sharding import PartitionSpec as P

HEADS = 12
NY = 4
ROWS = 16
MESH = pl.DeviceIdType.MESH
FAR = (False, True, True)
STEPS = (3.0, 4.0)
SHIFT = (7.0, 13.0)
SLOTS = (2.2, 1.1)
X_LAG = 5.0


def normal(values):
    mean = jnp.mean(values, axis=-1, keepdims=True)
    centred = values - mean
    var = jnp.mean(centred * centred, axis=-1, keepdims=True)
    return centred * lax.rsqrt(var + 1e-06)


def remote(source, target, send, arrive, device):
    return pltpu.make_async_remote_copy(
        src_ref=source,
        dst_ref=target,
        send_sem=send,
        recv_sem=arrive,
        device_id=device,
        device_id_type=MESH,
    )


def offsets(nz, c, t):
    up = nz // 2 if c % 2 == 0 else (nz - 1) // 2
    down = nz - 1 - up
    if t == 0:
        return [(0, (1,) * (up > 0) + (-1,) * (down > 0))]
    found = []
    if t <= up:
        found.append((nz - t, (1,) * (t < up)))
    if t <= down:
        found.append((t, (-1,) * (t < down)))
    return found


def schedule(nz, chunks):
    events = []
    y_free = begin = 0.0
    for c in range(chunks):
        far = FAR[c]
        last = 0.0
        for t in range(nz // 2 + 1):
            now = begin + t * STEPS[far]
            events.append((now, "near", c, t))
            if far:
                last = now + STEPS[far]
                events.append((last, "far", c, t))
            y_free = max(y_free, now)
            events.append((y_free, "slots", c, t))
            y_free += len(offsets(nz, c, t)) * SLOTS[far]
        begin += SHIFT[far]
        events.append((max(last, y_free + X_LAG), "hand", c, 0))
    rank = {"near": 0, "far": 1, "slots": 2, "hand": 3}
    return sorted(events, key=lambda e: (e[0], rank[e[1]], e[2], e[3]))


def project(c, sides, w_query, w_keyval, gains, query, keyval):
    chunks, count, rows, width = sides.shape
    f32, bf16 = jnp.float32, jnp.bfloat16
    pairs = count // 2
    for side in range(2):
        views = jnp.concatenate([sides[c, 2 * p + side] for p in range(pairs)], axis=0)
        level = normal(views.astype(f32))
        query_in = (level * gains[side, 0:1]).astype(bf16)
        found = jnp.dot(query_in, w_query[side], preferred_element_type=f32).astype(bf16)
        for p in range(pairs):
            query[2 * p + side, c * rows : (c + 1) * rows] = found[p * rows : (p + 1) * rows]
        memory_in = (level * gains[1 - side, 1:2]).astype(bf16)
        found = jnp.dot(memory_in, w_keyval[1 - side], preferred_element_type=f32).astype(bf16)
        for p in range(pairs):
            keyval[2 * p + 1 - side, c * rows : (c + 1) * rows] = found[p * rows : (p + 1) * rows]


def attend(i, sides, w_out, w_head, gains, query, keyval, context, ordered, out):
    chunks, count, rows, width = sides.shape
    tokv = chunks * rows
    size = width // HEADS
    scale = 1.4426950408889634 / size**0.5
    f32, bf16 = jnp.float32, jnp.bfloat16
    side = lax.rem(i, 2)
    gain = gains[side]
    lane = lax.broadcasted_iota(jnp.int32, (tokv, 2 * size), 1)
    first = lane < size
    ones = jnp.ones((tokv, 2 * size), bf16)
    for h in range(0, HEADS, 2):
        columns = slice(h * size, (h + 2) * size)
        both = query[i, :, columns]
        keys = keyval[i, :, columns]
        values = jnp.concatenate(
            [keyval[i, :, width + h * size : width + (h + 2) * size], ones], axis=1
        )
        found = []
        for half in range(2):
            mine = jnp.where(first if half == 0 else jnp.logical_not(first), both, jnp.zeros_like(both))
            scores = lax.dot_general(
                mine, keys, (((1,), (1,)), ((), ())), preferred_element_type=f32
            )
            top = jnp.max(scores, axis=-1, keepdims=True)
            probs = jnp.exp2((scores - top) * scale).astype(bf16)
            total = jnp.dot(probs, values, preferred_element_type=f32)
            found.append(total[:, : 2 * size] / total[:, 2 * size :])
        context[:, columns] = jnp.where(first, found[0], found[1]).astype(bf16)
    emb = jnp.concatenate([sides[c, i] for c in range(chunks)], axis=0)
    updated = emb.astype(f32) + jnp.dot(context[...], w_out[side], preferred_element_type=f32)
    final = (normal(updated) * gain[2:3]).astype(bf16)
    parts = rows // ROWS
    for c in range(chunks):
        for j in range(parts):
            place = (j * chunks + c) * ROWS
            come = (c * parts + j) * ROWS
            ordered[place : place + ROWS] = final[come : come + ROWS]
    head = lax.dot_general(
        w_head[side], ordered[...], (((1,), (1,)), ((), ())), preferred_element_type=f32
    )
    conf = 1.0 + jnp.exp(head[3:4])
    for c in range(4):
        record = conf * head[c : c + 1] if c < 3 else conf
        for b in range(tokv // 128):
            row = c * (tokv // 128) + b
            out[row // 2, pl.ds(row % 2 * count + i, 1), :] = record[:, b * 128 : (b + 1) * 128]


def kernel(nz, nm, chunks, *refs):
    refs = iter(refs)

    def take(n):
        return [next(refs) for unused in range(n)]

    tokens, wanted, places, spread, w_head, gains = take(6)
    in_hbm = take(4)
    (sums,) = take(1)
    w_embed, w_query, w_keyval, w_out = in_vmem = take(4)
    full, w_near, w_held, slots, parcels, sides = take(6)
    query, keyval, context, ordered, out, block, toward, came, mine_sum, every = take(10)
    pools = take(chunks)
    held = [take(nz) for unused in range(chunks)]
    distant = [take(nz) for unused in range(chunks)]
    (local, s1, r1, s2, r2, s3, r3, t_send, t_recv, w_send, w_recv) = take(11)
    (z_send, z_recv, p_send, p_recv, y_send, y_recv, x_send, x_recv) = take(8)

    view = lax.axis_index("view")
    me = lax.axis_index("mp")
    z = view // NY
    y = view % NY
    nv = nz * NY
    part = tokens.shape[1] // nm
    feat = tokens.shape[2]
    view_dev = tokens.shape[0]
    count = places.shape[0] // nm
    tokv = tokens.shape[1]

    def at_z(step):
        return (lax.rem(z + step + nz, nz) * NY + y, me)

    def at_y(step):
        return (z * NY + lax.rem(y + step + NY, NY), me)

    column_peers = [(view, lax.rem(me + o, nm)) for o in range(1, nm)]
    view_peers = [(lax.rem(view + o, nv), me) for o in range(1, nv)]
    barrier = pltpu.get_barrier_semaphore()
    for peer in column_peers + view_peers:
        pl.semaphore_signal(barrier, inc=1, device_id=peer, device_id_type=MESH)
    loads = [pltpu.make_async_copy(a, b, local.at[k]) for k, (a, b) in enumerate(zip(in_hbm, in_vmem))]
    loads[0].start()
    own = pltpu.make_async_copy(
        tokens.at[:, pl.ds(pl.multiple_of(me * part, ROWS), part), :],
        full.at[:, :, pl.ds(pl.multiple_of(me * feat, 128), feat)],
        local.at[4],
    )
    own.start()
    own_wanted = pltpu.make_async_copy(wanted, w_near.at[0], local.at[5])
    own_wanted.start()
    pl.semaphore_wait(barrier, nm + nv - 2)

    sent = []

    def start(copy):
        copy.start()
        sent.append(copy)
        return copy

    def receive(copies):
        for copy in copies:
            copy.wait_recv()

    arriving = []
    for o in range(1, nm):
        j = lax.rem(me + o, nm)
        arriving.append(
            start(
                remote(
                    tokens.at[:, pl.ds(pl.multiple_of(j * part, ROWS), part), :],
                    full.at[:, :, pl.ds(pl.multiple_of(me * feat, 128), feat)],
                    t_send.at[o],
                    t_recv.at[o],
                    column_peers[o - 1],
                )
            )
        )
    asking = [
        start(remote(wanted, w_near.at[NY - o], w_send.at[o], w_recv.at[NY - o], at_y(o)))
        for o in range(1, NY)
    ]
    for load in loads[1:]:
        load.start()
    own.wait()
    loads[0].wait()
    receive(arriving)
    emb = jnp.dot(
        full[...].reshape(view_dev * part, nm * feat), w_embed[...], preferred_element_type=jnp.float32
    )
    emb = emb.astype(jnp.bfloat16).reshape(view_dev, part, -1)
    for c in range(chunks):
        held[c][0][...] = emb[:, c * ROWS : (c + 1) * ROWS]

    z_copy, y_copy, x_copy, p_copy = {}, {}, {}, {}
    first_slot = [lax.rem(z + d, nz) * (NY * 2) for d in range(nz)]
    column_slot = [lax.rem(y + dy, NY) * 2 for dy in range(NY)]

    def choose(table, c, d, dy, dest, r):
        return table[c][d][w_held[dest, 0, first_slot[d] + column_slot[dy] + r]]

    def move(kind, table, c, d, ways):
        for way in ways:
            target = (d - way) % nz
            z_copy[kind, c, target] = start(
                remote(
                    table[c][d],
                    table[c][target],
                    z_send.at[c, kind, target],
                    z_recv.at[c, kind, target],
                    at_z(way),
                )
            )

    def near(c, t):
        for d, ways in offsets(nz, c, t):
            if t:
                z_copy[0, c, d].wait_recv()
            move(0, held, c, d, ways)
            if t == 0 and FAR[c]:
                p_copy[c] = start(remote(held[c][0], distant[c][0], p_send.at[c], p_recv.at[c], at_y(2)))

    def far(c, t):
        for d, ways in offsets(nz, c, t):
            (z_copy[1, c, d] if t else p_copy[c]).wait_recv()
            move(1, distant, c, d, ways)
        for d, ways in offsets(nz, c, t):
            for r in range(2):
                pools[c][4 * nz + 2 * d + r] = choose(distant, c, d, 2, 0, r)

    def send_slots(c, t):
        for d, unused in offsets(nz, c, t):
            for way, dest in enumerate((1, 3) if FAR[c] else (1, 3, 2)):
                for r in range(2):
                    slots[c, way, d, r] = choose(held, c, d, 0, dest, r)
                y_copy[c, way, d] = start(
                    remote(
                        slots.at[c, way, d],
                        pools[c].at[pl.ds(2 * nz * way + 2 * d, 2)],
                        y_send.at[c, way, d],
                        y_recv.at[c, way, d],
                        at_y(dest),
                    )
                )
            for r in range(2):
                pools[c][6 * nz + 2 * d + r] = choose(held, c, d, 0, 0, r)

    def hand(c, unused):
        receive([copy for key, copy in y_copy.items() if key[0] == c])
        rows = pl.ds(pl.multiple_of(me * ROWS, ROWS), ROWS)
        for o in range(1, nm):
            j = lax.rem(me + o, nm)
            for k in range(count):
                parcels[c, o, k] = pools[c][places[j * count + k]]
            x_copy[c, o] = start(
                remote(
                    parcels.at[c, o],
                    sides.at[c, :, rows, :],
                    x_send.at[c, o],
                    x_recv.at[c, o],
                    column_peers[o - 1],
                )
            )
        for k in range(count):
            sides[c, k, rows, :] = pools[c][places[me * count + k]]

    acts = {"near": near, "far": far, "slots": send_slots, "hand": hand}
    asked = False
    for unused, kind, c, t in schedule(nz, chunks):
        if not asked and kind in ("slots", "far"):
            asked = True
            own_wanted.wait()
            receive(asking)
            to_scalars = pltpu.make_async_copy(w_near, w_held, local.at[6])
            to_scalars.start()
            to_scalars.wait()
        acts[kind](c, t)
    for load in loads[1:]:
        load.wait()
    for c in range(chunks):
        receive([x_copy[c, o] for o in range(1, nm)])
        project(c, sides, w_query, w_keyval, gains, query, keyval)

    @pl.loop(0, count)
    def one_side(i):
        attend(i, sides, w_out, w_head, gains, query, keyval, context, ordered, out)

    receive(
        [
            start(remote(out.at[lax.rem(me + o, nm)], block.at[me], s1.at[o], r1.at[o], column_peers[o - 1]))
            for o in range(1, nm)
        ]
        + []
    )
    block[me] = out[me]
    toward[...] = jnp.dot(
        spread[...],
        block[...].reshape(nm * 8, 128),
        precision=lax.Precision.HIGHEST,
        preferred_element_type=jnp.float32,
    ).reshape(nv, 8, 128)
    came[view] = toward[view]
    receive(
        [
            start(remote(toward.at[lax.rem(view + o, nv)], came.at[view], s2.at[o], r2.at[o], view_peers[o - 1]))
            for o in range(1, nv)
        ]
    )
    mine_sum[...] = jnp.sum(came[...], axis=0)
    every[me] = mine_sum[...]
    receive(
        [
            start(remote(mine_sum, every.at[me], s3.at[o], r3.at[o], column_peers[o - 1]))
            for o in range(1, nm)
        ]
    )
    blocks = tokv // 128
    for index in range(view_dev):
        for row in range(4 * blocks):
            place = row % blocks * 128
            sums[index, row // blocks, place : place + 128] = every[row // 2, index * 2 + row % 2]
    for copy in sent:
        copy.wait_send()


def plan_sides(side_views, view_dev, cap):
    view_count = lax.axis_size("view")
    nz = view_count // NY
    me = lax.axis_index("view")
    count = side_views.shape[0]
    owners = side_views // view_dev
    positions = jnp.arange(count, dtype=jnp.int32)
    earlier = jnp.logical_and(
        owners[:, None] == owners[None, :], positions[None, :] < positions[:, None]
    )
    rank = jnp.sum(earlier, axis=1)
    slot_index = owners * cap + rank
    match = jnp.arange(128, dtype=jnp.int32)[:, None] == slot_index[None, :]
    wanted = jnp.sum(jnp.where(match, (side_views % view_dev)[None, :], 0), axis=1)
    wanted = jnp.broadcast_to(wanted[None, :], (8, 128))
    d = (owners // NY - me // NY + nz) % nz
    rel = (owners % NY - me % NY + NY) % NY
    base = jnp.where(rel == 0, 3, jnp.where(rel == 3, 0, jnp.where(rel == 1, 1, 2)))
    places = base * (2 * nz) + 2 * d + rank
    return wanted, places


def plan_spread(side_views, views, view_dev, nm):
    count = side_views.shape[0] // nm
    column = jnp.arange(nm * 2 * count, dtype=jnp.int32)
    row = jnp.arange(views * 2, dtype=jnp.int32)
    column_view = jnp.broadcast_to(side_views.reshape(nm, 1, count), (nm, 2, count)).reshape(-1)
    same = jnp.logical_and(
        row[:, None] // 2 == column_view[None, :], row[:, None] % 2 == (column // count % 2)[None, :]
    )
    return same.astype(jnp.float32)


def on_device(tokens, pairs, w_embed, w_query, w_keyval, w_out, w_head, gains):
    nv = lax.axis_size("view")
    nm = lax.axis_size("mp")
    nz = nv // NY
    view_dev, tokv, feat = tokens.shape
    width = w_embed.shape[1]
    sides_all = 2 * pairs.shape[0]
    count = sides_all // nm
    side_views = pairs.reshape(sides_all)
    wanted, places = plan_sides(side_views, view_dev, 2)
    spread = plan_spread(side_views, nv * view_dev, view_dev, nm)
    part = tokv // nm
    chunks = part // ROWS
    piece = (ROWS, width)
    f32, bf16, i32 = jnp.float32, jnp.bfloat16, jnp.int32
    vmem = pl.BlockSpec(memory_space=pltpu.VMEM)
    hbm = pl.BlockSpec(memory_space=pltpu.HBM)
    dma = pltpu.SemaphoreType.DMA
    weights = (w_embed, w_query, w_keyval, w_out)
    return pl.pallas_call(
        functools.partial(kernel, nz, nm, chunks),
        out_shape=jax.ShapeDtypeStruct((view_dev, 4, tokv), f32),
        in_specs=[hbm, vmem, pl.BlockSpec(memory_space=pltpu.SMEM), vmem, vmem, vmem] + [hbm] * 4,
        out_specs=vmem,
        scratch_shapes=[pltpu.VMEM(w.shape, bf16) for w in weights]
        + [
            pltpu.VMEM((view_dev, part, nm * feat), bf16),
            pltpu.VMEM((NY,) + wanted.shape, i32),
            pltpu.SMEM((NY,) + wanted.shape, i32),
            pltpu.VMEM((chunks, 3, nz, 2) + piece, bf16),
            pltpu.VMEM((chunks, nm, count) + piece, bf16),
            pltpu.VMEM((chunks, count, nm * ROWS, width), bf16),
            pltpu.VMEM((count, tokv, width), bf16),
            pltpu.VMEM((count, tokv, 2 * width), bf16),
            pltpu.VMEM((tokv, width), bf16),
            pltpu.VMEM((tokv, width), bf16),
            pltpu.VMEM((nm, 8, 128), f32),
            pltpu.VMEM((nm, 8, 128), f32),
            pltpu.VMEM((nv, 8, 128), f32),
            pltpu.VMEM((nv, 8, 128), f32),
            pltpu.VMEM((8, 128), f32),
            pltpu.VMEM((nm, 8, 128), f32),
        ]
        + [pltpu.VMEM((8 * nz,) + piece, bf16)] * chunks
        + [pltpu.VMEM((view_dev,) + piece, bf16)] * (2 * chunks * nz)
        + [dma((7,))]
        + [dma((nm,))] * 2
        + [dma((nv,))] * 2
        + [dma((nm,))] * 4
        + [dma((NY,))] * 2
        + [dma((chunks, 2, nz))] * 2
        + [dma((chunks,))] * 2
        + [dma((chunks, 3, nz))] * 2
        + [dma((chunks, nm))] * 2,
        compiler_params=pltpu.CompilerParams(
            collective_id=0, has_side_effects=True, vmem_limit_bytes=60 * 2**20
        ),
    )(tokens, wanted, places, spread, w_head, gains, *weights)


def solution(mesh):
    return jax.shard_map(
        on_device,
        mesh=mesh,
        in_specs=(P("view", None, "mp"), P("view", None), P(), P(), P(), P(), P(), P()),
        out_specs=P("view", None, None),
        check_vma=False,
    )
```

```python
import functools

import jax
import jax.numpy as jnp
from jax import lax
from jax.experimental import pallas as pl
from jax.experimental.pallas import tpu as pltpu
from jax.sharding import PartitionSpec as P

HEADS = 12
NY = 4
ROWS = 16
MESH = pl.DeviceIdType.MESH
FAR = (False, True, True)
ORDER = (
    (0, 0, 0),
    (0, 0, 1),
    (0, 1, 0),
    (0, 0, 2),
    (1, 0, 1),
    (1, 1, 0),
    (0, 1, 1),
    (0, 0, 3),
    (1, 0, 0),
    (1, 0, 2),
    (0, 1, 2),
    (1, 0, 3),
    (0, 0, 4),
    (0, 2, 0),
    (1, 0, 4),
    (0, 1, 3),
    (1, 1, 2),
    (1, 2, 0),
    (0, 2, 1),
    (1, 1, 3),
    (2, 0, 0),
    (1, 1, 1),
    (0, 1, 4),
    (1, 1, 4),
    (1, 2, 1),
    (0, 2, 2),
    (1, 2, 2),
    (2, 1, 0),
    (0, 2, 3),
    (1, 2, 3),
    (0, 2, 4),
    (1, 2, 4),
    (2, 2, 0),
)


def normal(values):
    mean = jnp.mean(values, axis=-1, keepdims=True)
    centred = values - mean
    var = jnp.mean(centred * centred, axis=-1, keepdims=True)
    return centred * lax.rsqrt(var + 1e-06)


def remote(source, target, send, arrive, device):
    return pltpu.make_async_remote_copy(
        src_ref=source,
        dst_ref=target,
        send_sem=send,
        recv_sem=arrive,
        device_id=device,
        device_id_type=MESH,
    )


def offsets(nz, c, t):
    up = nz // 2 if c % 2 == 0 else (nz - 1) // 2
    down = nz - 1 - up
    if t == 0:
        return [(0, (1,) * (up > 0) + (-1,) * (down > 0))]
    found = []
    if t <= up:
        found.append((nz - t, (1,) * (t < up)))
    if t <= down:
        found.append((t, (-1,) * (t < down)))
    return found


def position(nz, d):
    return 0 if d == 0 else 2 * d if d < nz - d else 2 * (nz - d) - 1


def project(c, sides, w_query, w_keyval, gains, query, keyval):
    chunks, count, rows, width = sides.shape
    f32, bf16 = jnp.float32, jnp.bfloat16
    pairs = count // 2
    for side in range(2):
        views = jnp.concatenate([sides[c, 2 * p + side] for p in range(pairs)], axis=0)
        level = normal(views.astype(f32))
        query_in = (level * gains[0, side : side + 1]).astype(bf16)
        found = jnp.dot(query_in, w_query[side], preferred_element_type=f32).astype(bf16)
        for p in range(pairs):
            query[2 * p + side, c * rows : (c + 1) * rows] = found[p * rows : (p + 1) * rows]
        memory_in = (level * gains[1, 1 - side : 2 - side]).astype(bf16)
        found = jnp.dot(memory_in, w_keyval[1 - side], preferred_element_type=f32).astype(bf16)
        for p in range(pairs):
            keyval[2 * p + 1 - side, c * rows : (c + 1) * rows] = found[p * rows : (p + 1) * rows]


def attend(i, sides, w_out, w_head, gains, query, keyval, context, ordered, out):
    chunks, count, rows, width = sides.shape
    tokv = chunks * rows
    size = width // HEADS
    scale = 1.4426950408889634 / size**0.5
    f32, bf16 = jnp.float32, jnp.bfloat16
    side = lax.rem(i, 2)
    lane = lax.broadcasted_iota(jnp.int32, (tokv, 2 * size), 1)
    first = lane < size
    zero = jnp.zeros((tokv, 2 * size), bf16)
    ones = jnp.ones((tokv, 2 * size), bf16)
    counts = jnp.concatenate([jnp.where(first, ones, zero), jnp.where(first, zero, ones)], axis=0)

    def stack(columns):
        both = keyval[i, :, columns]
        return jnp.concatenate([jnp.where(first, both, zero), jnp.where(first, zero, both)], axis=0)

    def score(h):
        columns = slice(h * size, (h + 2) * size)
        return lax.dot_general(
            query[i, :, columns], stack(columns), (((1,), (1,)), ((), ())), preferred_element_type=f32
        )

    ahead = score(0)
    for h in range(0, HEADS, 2):
        scores = ahead
        if h + 2 < HEADS:
            ahead = score(h + 2)
        probs = []
        for half in range(2):
            own = scores[:, half * tokv : (half + 1) * tokv]
            top = jnp.max(own, axis=-1, keepdims=True)
            probs.append(jnp.exp2((own - top) * scale).astype(bf16))
        values = stack(slice(width + h * size, width + (h + 2) * size))
        total = jnp.dot(
            jnp.concatenate(probs, axis=1),
            jnp.concatenate([values, counts], axis=1),
            preferred_element_type=f32,
        )
        context[:, h * size : (h + 2) * size] = (total[:, : 2 * size] / total[:, 2 * size :]).astype(bf16)
    emb = jnp.concatenate([sides[c, i] for c in range(chunks)], axis=0)
    updated = emb.astype(f32) + jnp.dot(context[...], w_out[side], preferred_element_type=f32)
    final = (normal(updated) * gains[2, pl.ds(side, 1)]).astype(bf16)
    parts = rows // ROWS
    for c in range(chunks):
        for j in range(parts):
            place = (j * chunks + c) * ROWS
            come = (c * parts + j) * ROWS
            ordered[place : place + ROWS] = final[come : come + ROWS]
    head = lax.dot_general(
        w_head[side], ordered[...], (((1,), (1,)), ((), ())), preferred_element_type=f32
    )
    conf = 1.0 + jnp.exp(head[3:4])
    for c in range(4):
        record = conf * head[c : c + 1] if c < 3 else conf
        for b in range(tokv // 128):
            row = c * (tokv // 128) + b
            out[row // 2, pl.ds(row % 2 * count + i, 1), :] = record[:, b * 128 : (b + 1) * 128]


def plan(nz, count, view_dev, z, y, pairs, wanted, keys, places):
    total = 2 * pairs.shape[1]
    shape = wanted.shape
    lane = lax.broadcasted_iota(jnp.int32, shape, 1)
    views = [pairs[k % 2, k // 2] for k in range(total)]
    bits = view_dev.bit_length() - 1
    owners = [lax.shift_right_logical(v, bits) for v in views]
    asks = jnp.zeros(shape, jnp.int32)
    labels = jnp.zeros(shape, jnp.int32)
    for k in range(total):
        rank = jnp.int32(0)
        for j in range(k):
            rank = jnp.where(owners[j] == owners[k], 1, rank)
        asks = jnp.where(lane == owners[k] * 2 + rank, views[k] & (view_dev - 1), asks)
        for sub in range(2):
            spot = k // count * 2 * count + sub * count + k % count
            labels = jnp.where(lane == spot, views[k] * 2 + sub, labels)
        d = (lax.shift_right_logical(owners[k], NY.bit_length() - 1) - z + nz) & (nz - 1)
        come = (owners[k] - y + NY) & (NY - 1)
        base = jnp.where(come == 0, 3, jnp.where(come == NY - 1, 0, come))
        spot = jnp.where(d == 0, 0, jnp.where(2 * d < nz, 2 * d, 2 * (nz - d) - 1))
        places[k] = base * (2 * nz) + 2 * spot + rank
    wanted[...] = asks
    keys[...] = labels


def kernel(nz, nm, chunks, *refs):
    refs = iter(refs)

    def take(n):
        return [next(refs) for unused in range(n)]

    tokens, pairs, w_head, gains = take(4)
    in_hbm = take(4)
    (sums,) = take(1)
    w_embed, w_query, w_keyval, w_out = in_vmem = take(4)
    wanted, keys, places, full, w_near, w_held, slots, parcels, sides = take(9)
    query, keyval, context, ordered, out, block, toward, came, half, came_y, mine_sum, every = take(12)
    pools = take(chunks)
    held = [take(nz) for unused in range(chunks)]
    (local, s1, r1, s2, r2, s4, r4, s3, r3, t_send, t_recv, w_send, w_recv) = take(13)
    (z_send, z_recv, p_send, p_recv, y_send, y_recv, x_send, x_recv) = take(8)

    view = lax.axis_index("view")
    me = lax.axis_index("mp")
    z = view // NY
    y = view % NY
    nv = nz * NY
    part = tokens.shape[1] // nm
    feat = tokens.shape[2]
    view_dev = tokens.shape[0]
    total = 2 * pairs.shape[1]
    count = total // nm
    tokv = tokens.shape[1]

    def at_z(step):
        return (lax.rem(z + step + nz, nz) * NY + y, me)

    def at_y(step):
        return (z * NY + lax.rem(y + step + NY, NY), me)

    column_peers = [(view, lax.rem(me + o, nm)) for o in range(1, nm)]
    peers = column_peers + [at_z(o) for o in range(1, nz)] + [at_y(o) for o in range(1, NY)]
    barrier = pltpu.get_barrier_semaphore()
    for peer in peers:
        pl.semaphore_signal(barrier, inc=1, device_id=peer, device_id_type=MESH)
    loads = [pltpu.make_async_copy(a, b, local.at[k]) for k, (a, b) in enumerate(zip(in_hbm, in_vmem))]
    loads[0].start()
    own = pltpu.make_async_copy(
        tokens.at[:, pl.ds(pl.multiple_of(me * part, ROWS), part), :],
        full.at[:, :, pl.ds(pl.multiple_of(me * feat, 128), feat)],
        local.at[4],
    )
    own.start()
    plan(nz, count, view_dev, z, y, pairs, wanted, keys, places)
    w_near[0] = wanted[...]
    pl.semaphore_wait(barrier, len(peers))

    sent = []

    def start(copy):
        copy.start()
        sent.append(copy)
        return copy

    def finish(keep=0):
        for copy in sent[: len(sent) - keep]:
            copy.wait_send()
        del sent[: len(sent) - keep]

    def receive(copies):
        for copy in copies:
            copy.wait_recv()

    arriving = []
    for o in range(1, nm):
        j = lax.rem(me + o, nm)
        arriving.append(
            start(
                remote(
                    tokens.at[:, pl.ds(pl.multiple_of(j * part, ROWS), part), :],
                    full.at[:, :, pl.ds(pl.multiple_of(me * feat, 128), feat)],
                    t_send.at[o],
                    t_recv.at[o],
                    column_peers[o - 1],
                )
            )
        )
    asking = [
        start(remote(wanted, w_near.at[NY - o], w_send.at[o], w_recv.at[NY - o], at_y(o)))
        for o in range(1, NY)
    ]
    for load in loads[1:]:
        load.start()
    own.wait()
    loads[0].wait()
    receive(arriving)
    emb = jnp.dot(
        full[...].reshape(view_dev * part, nm * feat), w_embed[...], preferred_element_type=jnp.float32
    )
    emb = emb.astype(jnp.bfloat16).reshape(view_dev, part, -1)
    for c in range(chunks):
        held[c][0][0:view_dev] = emb[:, c * ROWS : (c + 1) * ROWS]

    z_copy, y_copy, x_copy = {}, {}, {}
    p_copy = {
        c: start(
            remote(
                held[c][0].at[pl.ds(0, view_dev)],
                held[c][0].at[pl.ds(view_dev, view_dev)],
                p_send.at[c],
                p_recv.at[c],
                at_y(2),
            )
        )
        for c in range(chunks)
        if FAR[c]
    }
    first_slot = [lax.rem(z + d, nz) * (NY * 2) for d in range(nz)]
    column_slot = [lax.rem(y + dy, NY) * 2 for dy in range(NY)]

    def choose(c, d, column, dest, r):
        local = w_held[dest, 0, first_slot[d] + column_slot[column] + r]
        return held[c][d][local if column == 0 else local + view_dev]

    def near(c, t):
        if t == 0 and FAR[c]:
            p_copy[c].wait_recv()
        for d, ways in offsets(nz, c, t):
            if t:
                z_copy[c, d].wait_recv()
            for way in ways:
                target = (d - way) % nz
                z_copy[c, target] = start(
                    remote(
                        held[c][d],
                        held[c][target],
                        z_send.at[c, target],
                        z_recv.at[c, target],
                        at_z(way),
                    )
                )

    def send_slots(c, t):
        found = [d for d, unused in offsets(nz, c, t)]
        low = 2 * min(position(nz, d) for d in found)
        for way, dest in enumerate((1, 3) if FAR[c] else (1, 3, 2)):
            for d in found:
                for r in range(2):
                    slots[c, way, 2 * position(nz, d) + r] = choose(c, d, 0, dest, r)
            y_copy[c, way, t] = start(
                remote(
                    slots.at[c, way, pl.ds(low, 2 * len(found))],
                    pools[c].at[pl.ds(2 * nz * way + low, 2 * len(found))],
                    y_send.at[c, way, t],
                    y_recv.at[c, way, t],
                    at_y(dest),
                )
            )
        for d in found:
            for r in range(2):
                pools[c][6 * nz + 2 * position(nz, d) + r] = choose(c, d, 0, 0, r)
                if FAR[c]:
                    pools[c][4 * nz + 2 * position(nz, d) + r] = choose(c, d, 2, 0, r)

    def hand(c, unused):
        receive([copy for key, copy in y_copy.items() if key[0] == c])
        rows = pl.ds(pl.multiple_of(me * ROWS, ROWS), ROWS)
        for o in range(1, nm):
            j = lax.rem(me + o, nm)
            for k in range(count):
                parcels[c, o, k] = pools[c][places[j * count + k]]
            x_copy[c, o] = start(
                remote(
                    parcels.at[c, o],
                    sides.at[c, :, rows, :],
                    x_send.at[c, o],
                    x_recv.at[c, o],
                    column_peers[o - 1],
                )
            )
        for k in range(count):
            sides[c, k, rows, :] = pools[c][places[me * count + k]]

    acts = (near, send_slots, hand)
    asked = False
    for kind, c, t in ORDER:
        if not asked and kind == 1:
            asked = True
            receive(asking)
            to_scalars = pltpu.make_async_copy(w_near, w_held, local.at[6])
            to_scalars.start()
            to_scalars.wait()
        acts[kind](c, t)
    for load in loads[1:]:
        load.wait()
    finish(keep=nm - 1)
    for c in range(chunks):
        receive([x_copy[c, o] for o in range(1, nm)])
        project(c, sides, w_query, w_keyval, gains, query, keyval)

    @pl.loop(0, count)
    def one_side(i):
        attend(i, sides, w_out, w_head, gains, query, keyval, context, ordered, out)

    receive(
        [
            start(remote(out.at[lax.rem(me + o, nm)], block.at[me], s1.at[o], r1.at[o], column_peers[o - 1]))
            for o in range(1, nm)
        ]
    )
    block[me] = out[me]
    row = lax.broadcasted_iota(jnp.int32, (nv * 8, nm * 8), 0)
    toward[...] = jnp.dot(
        jnp.where(row == keys[0:1, 0 : nm * 8], 1.0, 0.0),
        block[...].reshape(nm * 8, 128),
        precision=lax.Precision.HIGHEST,
        preferred_element_type=jnp.float32,
    ).reshape(nv, 8, 128)
    came[z] = toward[pl.ds(z * NY, NY)]
    receive(
        [
            start(
                remote(
                    toward.at[pl.ds(lax.rem(z + o, nz) * NY, NY)], came.at[z], s2.at[o], r2.at[o], at_z(o)
                )
            )
            for o in range(1, nz)
        ]
    )
    half[...] = jnp.sum(came[...], axis=0)
    came_y[y] = half[y]
    receive(
        [
            start(remote(half.at[lax.rem(y + o, NY)], came_y.at[y], s4.at[o], r4.at[o], at_y(o)))
            for o in range(1, NY)
        ]
    )
    mine_sum[...] = jnp.sum(came_y[...], axis=0)
    every[me] = mine_sum[...]
    receive(
        [
            start(remote(mine_sum, every.at[me], s3.at[o], r3.at[o], column_peers[o - 1]))
            for o in range(1, nm)
        ]
    )
    blocks = tokv // 128
    for index in range(view_dev):
        for row in range(4 * blocks):
            place = row % blocks * 128
            sums[index, row // blocks, place : place + 128] = every[row // 2, index * 2 + row % 2]
    finish()


def on_device(tokens, pairs, w_embed, w_query, w_keyval, w_out, w_head, gains):
    nv = lax.axis_size("view")
    nm = lax.axis_size("mp")
    nz = nv // NY
    view_dev, tokv, feat = tokens.shape
    width = w_embed.shape[1]
    count = 2 * pairs.shape[0] // nm
    ask = (8, 128)
    part = tokv // nm
    chunks = part // ROWS
    piece = (ROWS, width)
    f32, bf16, i32 = jnp.float32, jnp.bfloat16, jnp.int32
    vmem = pl.BlockSpec(memory_space=pltpu.VMEM)
    hbm = pl.BlockSpec(memory_space=pltpu.HBM)
    dma = pltpu.SemaphoreType.DMA
    weights = (w_embed, w_query, w_keyval, w_out)
    return pl.pallas_call(
        functools.partial(kernel, nz, nm, chunks),
        out_shape=jax.ShapeDtypeStruct((view_dev, 4, tokv), f32),
        in_specs=[hbm, pl.BlockSpec(memory_space=pltpu.SMEM), vmem, vmem] + [hbm] * 4,
        out_specs=vmem,
        scratch_shapes=[pltpu.VMEM(w.shape, bf16) for w in weights]
        + [
            pltpu.VMEM(ask, i32),
            pltpu.VMEM(ask, i32),
            pltpu.SMEM((2 * pairs.shape[0],), i32),
            pltpu.VMEM((view_dev, part, nm * feat), bf16),
            pltpu.VMEM((NY,) + ask, i32),
            pltpu.SMEM((NY,) + ask, i32),
            pltpu.VMEM((chunks, 3, 2 * nz) + piece, bf16),
            pltpu.VMEM((chunks, nm, count) + piece, bf16),
            pltpu.VMEM((chunks, count, nm * ROWS, width), bf16),
            pltpu.VMEM((count, tokv, width), bf16),
            pltpu.VMEM((count, tokv, 2 * width), bf16),
            pltpu.VMEM((tokv, width), bf16),
            pltpu.VMEM((tokv, width), bf16),
            pltpu.VMEM((nm, 8, 128), f32),
            pltpu.VMEM((nm, 8, 128), f32),
            pltpu.VMEM((nv, 8, 128), f32),
            pltpu.VMEM((nz, NY, 8, 128), f32),
            pltpu.VMEM((NY, 8, 128), f32),
            pltpu.VMEM((NY, 8, 128), f32),
            pltpu.VMEM((8, 128), f32),
            pltpu.VMEM((nm, 8, 128), f32),
        ]
        + [pltpu.VMEM((8 * nz,) + piece, bf16)] * chunks
        + [
            pltpu.VMEM(((2 if FAR[c] else 1) * view_dev,) + piece, bf16)
            for c in range(chunks)
            for unused in range(nz)
        ]
        + [dma((7,))]
        + [dma((nm,))] * 2
        + [dma((nz,))] * 2
        + [dma((NY,))] * 2
        + [dma((nm,))] * 4
        + [dma((NY,))] * 2
        + [dma((chunks, nz))] * 2
        + [dma((chunks,))] * 2
        + [dma((chunks, 3, nz // 2 + 1))] * 2
        + [dma((chunks, nm))] * 2,
        compiler_params=pltpu.CompilerParams(
            collective_id=0, has_side_effects=True, vmem_limit_bytes=60 * 2**20
        ),
    )(tokens, pairs.T, w_head, jnp.transpose(gains, (1, 0, 2)), *weights)


def solution(mesh):
    return jax.shard_map(
        on_device,
        mesh=mesh,
        in_specs=(P("view", None, "mp"), P("view", None), P(), P(), P(), P(), P(), P()),
        out_specs=P("view", None, None),
        check_vma=False,
    )
```

```python
import functools

import jax
import jax.numpy as jnp
from jax import lax
from jax.experimental import pallas as pl
from jax.experimental.pallas import tpu as pltpu
from jax.sharding import PartitionSpec as P

HEADS = 12
NY = 4
ROWS = 16
MESH = pl.DeviceIdType.MESH
FAR = (False, False, True)
ORDER = (
    (0, 0, 0),
    (0, 1, 0),
    (1, 0, 0),
    (0, 0, 1),
    (1, 0, 1),
    (0, 1, 1),
    (1, 1, 1),
    (0, 0, 2),
    (0, 1, 2),
    (0, 0, 3),
    (0, 2, 0),
    (1, 0, 2),
    (1, 0, 3),
    (0, 1, 3),
    (0, 2, 1),
    (0, 0, 4),
    (1, 0, 4),
    (1, 1, 0),
    (1, 1, 2),
    (0, 1, 4),
    (0, 2, 2),
    (2, 0, 0),
    (1, 1, 4),
    (1, 1, 3),
    (0, 2, 3),
    (1, 2, 2),
    (1, 2, 3),
    (0, 2, 4),
    (1, 2, 4),
    (2, 1, 0),
    (1, 2, 1),
    (1, 2, 0),
    (2, 2, 0),
)


def normal(values):
    mean = jnp.mean(values, axis=-1, keepdims=True)
    centred = values - mean
    var = jnp.mean(centred * centred, axis=-1, keepdims=True)
    return centred * lax.rsqrt(var + 1e-06)


def remote(source, target, send, arrive, device):
    return pltpu.make_async_remote_copy(
        src_ref=source,
        dst_ref=target,
        send_sem=send,
        recv_sem=arrive,
        device_id=device,
        device_id_type=MESH,
    )


def offsets(nz, c, t):
    up = nz // 2 if c % 2 == 0 else (nz - 1) // 2
    down = nz - 1 - up
    if t == 0:
        return [(0, (1,) * (up > 0) + (-1,) * (down > 0))]
    found = []
    if t <= up:
        found.append((nz - t, (1,) * (t < up)))
    if t <= down:
        found.append((t, (-1,) * (t < down)))
    return found


def position(nz, d):
    return 0 if d == 0 else 2 * d if d < nz - d else 2 * (nz - d) - 1


def project(c, sides, w_query, w_keyval, gains, query, keyval):
    chunks, count, rows, width = sides.shape
    f32, bf16 = jnp.float32, jnp.bfloat16
    pairs = count // 2
    for side in range(2):
        views = jnp.concatenate([sides[c, 2 * p + side] for p in range(pairs)], axis=0)
        level = normal(views.astype(f32))
        query_in = (level * gains[0, side : side + 1]).astype(bf16)
        found = jnp.dot(query_in, w_query[side], preferred_element_type=f32).astype(bf16)
        for p in range(pairs):
            query[2 * p + side, c * rows : (c + 1) * rows] = found[p * rows : (p + 1) * rows]
        memory_in = (level * gains[1, 1 - side : 2 - side]).astype(bf16)
        found = jnp.dot(memory_in, w_keyval[1 - side], preferred_element_type=f32).astype(bf16)
        for p in range(pairs):
            keyval[2 * p + 1 - side, c * rows : (c + 1) * rows] = found[p * rows : (p + 1) * rows]


def attend(i, sides, w_out, w_head, gains, query, keyval, context, ordered, out):
    chunks, count, rows, width = sides.shape
    tokv = chunks * rows
    size = width // HEADS
    scale = 1.4426950408889634 / size**0.5
    f32, bf16 = jnp.float32, jnp.bfloat16
    side = lax.rem(i, 2)
    lane = lax.broadcasted_iota(jnp.int32, (tokv, 2 * size), 1)
    first = lane < size
    zero = jnp.zeros((tokv, 2 * size), bf16)
    ones = jnp.ones((tokv, 2 * size), bf16)
    counts = jnp.concatenate([jnp.where(first, ones, zero), jnp.where(first, zero, ones)], axis=0)

    def stack(columns):
        both = keyval[i, :, columns]
        return jnp.concatenate([jnp.where(first, both, zero), jnp.where(first, zero, both)], axis=0)

    def score(h):
        columns = slice(h * size, (h + 2) * size)
        return lax.dot_general(
            query[i, :, columns], stack(columns), (((1,), (1,)), ((), ())), preferred_element_type=f32
        )

    ahead = score(0)
    for h in range(0, HEADS, 2):
        scores = ahead
        if h + 2 < HEADS:
            ahead = score(h + 2)
        probs = []
        for half in range(2):
            own = scores[:, half * tokv : (half + 1) * tokv]
            top = jnp.max(own, axis=-1, keepdims=True)
            probs.append(jnp.exp2((own - top) * scale).astype(bf16))
        values = stack(slice(width + h * size, width + (h + 2) * size))
        total = jnp.dot(
            jnp.concatenate(probs, axis=1),
            jnp.concatenate([values, counts], axis=1),
            preferred_element_type=f32,
        )
        context[:, h * size : (h + 2) * size] = (total[:, : 2 * size] / total[:, 2 * size :]).astype(bf16)
    emb = jnp.concatenate([sides[c, i] for c in range(chunks)], axis=0)
    updated = emb.astype(f32) + jnp.dot(context[...], w_out[side], preferred_element_type=f32)
    final = (normal(updated) * gains[2, pl.ds(side, 1)]).astype(bf16)
    parts = rows // ROWS
    for c in range(chunks):
        for j in range(parts):
            place = (j * chunks + c) * ROWS
            come = (c * parts + j) * ROWS
            ordered[place : place + ROWS] = final[come : come + ROWS]
    head = lax.dot_general(
        w_head[side], ordered[...], (((1,), (1,)), ((), ())), preferred_element_type=f32
    )
    conf = 1.0 + jnp.exp(head[3:4])
    for c in range(4):
        record = conf * head[c : c + 1] if c < 3 else conf
        for b in range(tokv // 128):
            row = c * (tokv // 128) + b
            out[row // 2, pl.ds(row % 2 * count + i, 1), :] = record[:, b * 128 : (b + 1) * 128]


def plan(nz, count, view_dev, z, y, pairs, wanted, keys, places):
    total = 2 * pairs.shape[1]
    shape = wanted.shape
    lane = lax.broadcasted_iota(jnp.int32, shape, 1)
    views = [pairs[k % 2, k // 2] for k in range(total)]
    bits = view_dev.bit_length() - 1
    owners = [lax.shift_right_logical(v, bits) for v in views]
    asks = jnp.zeros(shape, jnp.int32)
    labels = jnp.zeros(shape, jnp.int32)
    for k in range(total):
        rank = jnp.int32(0)
        for j in range(k):
            rank = jnp.where(owners[j] == owners[k], 1, rank)
        asks = jnp.where(lane == owners[k] * 2 + rank, views[k] & (view_dev - 1), asks)
        for sub in range(2):
            spot = k // count * 2 * count + sub * count + k % count
            labels = jnp.where(lane == spot, views[k] * 2 + sub, labels)
        d = (lax.shift_right_logical(owners[k], NY.bit_length() - 1) - z + nz) & (nz - 1)
        come = (owners[k] - y + NY) & (NY - 1)
        base = jnp.where(come == 0, 3, jnp.where(come == NY - 1, 0, come))
        spot = jnp.where(d == 0, 0, jnp.where(2 * d < nz, 2 * d, 2 * (nz - d) - 1))
        places[k] = base * (2 * nz) + 2 * spot + rank
    wanted[...] = asks
    keys[...] = labels


def kernel(nz, nm, chunks, *refs):
    refs = iter(refs)

    def take(n):
        return [next(refs) for unused in range(n)]

    tokens, pairs, w_head, gains = take(4)
    in_hbm = take(4)
    (sums,) = take(1)
    w_embed, w_query, w_keyval, w_out = in_vmem = take(4)
    wanted, keys, places, full, w_near, w_held, slots, parcels, sides = take(9)
    query, keyval, context, ordered, out, block, toward, came, half, came_y, mine_sum, every = take(12)
    pools = take(chunks)
    held = [take(nz) for unused in range(chunks)]
    (local, s1, r1, s2, r2, s4, r4, s3, r3, t_send, t_recv, w_send, w_recv) = take(13)
    (z_send, z_recv, p_send, p_recv, y_send, y_recv, x_send, x_recv) = take(8)

    view = lax.axis_index("view")
    me = lax.axis_index("mp")
    z = view // NY
    y = view % NY
    nv = nz * NY
    part = tokens.shape[1] // nm
    feat = tokens.shape[2]
    view_dev = tokens.shape[0]
    total = 2 * pairs.shape[1]
    count = total // nm
    tokv = tokens.shape[1]

    def at_z(step):
        return (lax.rem(z + step + nz, nz) * NY + y, me)

    def at_y(step):
        return (z * NY + lax.rem(y + step + NY, NY), me)

    column_peers = [(view, lax.rem(me + o, nm)) for o in range(1, nm)]
    peers = column_peers + [at_z(o) for o in range(1, nz)] + [at_y(o) for o in range(1, NY)]
    barrier = pltpu.get_barrier_semaphore()
    for peer in peers:
        pl.semaphore_signal(barrier, inc=1, device_id=peer, device_id_type=MESH)
    loads = [pltpu.make_async_copy(a, b, local.at[k]) for k, (a, b) in enumerate(zip(in_hbm, in_vmem))]
    loads[0].start()
    own = pltpu.make_async_copy(
        tokens.at[:, pl.ds(pl.multiple_of(me * part, ROWS), part), :],
        full.at[:, :, pl.ds(pl.multiple_of(me * feat, 128), feat)],
        local.at[4],
    )
    own.start()
    plan(nz, count, view_dev, z, y, pairs, wanted, keys, places)
    w_near[0] = wanted[...]
    pl.semaphore_wait(barrier, len(peers))

    sent = []

    def start(copy):
        copy.start()
        sent.append(copy)
        return copy

    def finish(keep=0):
        for copy in sent[: len(sent) - keep]:
            copy.wait_send()
        del sent[: len(sent) - keep]

    def receive(copies):
        for copy in copies:
            copy.wait_recv()

    arriving = []
    for o in range(1, nm):
        j = lax.rem(me + o, nm)
        arriving.append(
            start(
                remote(
                    tokens.at[:, pl.ds(pl.multiple_of(j * part, ROWS), part), :],
                    full.at[:, :, pl.ds(pl.multiple_of(me * feat, 128), feat)],
                    t_send.at[o],
                    t_recv.at[o],
                    column_peers[o - 1],
                )
            )
        )
    asking = [
        start(remote(wanted, w_near.at[NY - o], w_send.at[o], w_recv.at[NY - o], at_y(o)))
        for o in range(1, NY)
    ]
    for load in loads[1:]:
        load.start()
    own.wait()
    loads[0].wait()
    receive(arriving)
    emb = jnp.dot(
        full[...].reshape(view_dev * part, nm * feat), w_embed[...], preferred_element_type=jnp.float32
    )
    emb = emb.astype(jnp.bfloat16).reshape(view_dev, part, -1)
    for c in range(chunks):
        held[c][0][0:view_dev] = emb[:, c * ROWS : (c + 1) * ROWS]

    z_copy, y_copy, x_copy = {}, {}, {}
    p_copy = {
        c: start(
            remote(
                held[c][0].at[pl.ds(0, view_dev)],
                held[c][0].at[pl.ds(view_dev, view_dev)],
                p_send.at[c],
                p_recv.at[c],
                at_y(2),
            )
        )
        for c in range(chunks)
        if FAR[c]
    }
    first_slot = [lax.rem(z + d, nz) * (NY * 2) for d in range(nz)]
    column_slot = [lax.rem(y + dy, NY) * 2 for dy in range(NY)]

    def choose(c, d, column, dest, r):
        local = w_held[dest, 0, first_slot[d] + column_slot[column] + r]
        return held[c][d][local if column == 0 else local + view_dev]

    def near(c, t):
        if t == 0 and FAR[c]:
            p_copy[c].wait_recv()
        for d, ways in offsets(nz, c, t):
            if t:
                z_copy[c, d].wait_recv()
            for way in ways:
                target = (d - way) % nz
                z_copy[c, target] = start(
                    remote(
                        held[c][d],
                        held[c][target],
                        z_send.at[c, target],
                        z_recv.at[c, target],
                        at_z(way),
                    )
                )

    def send_slots(c, t):
        found = [d for d, unused in offsets(nz, c, t)]
        low = 2 * min(position(nz, d) for d in found)
        for way, dest in enumerate((1, 3) if FAR[c] else (1, 3, 2)):
            for d in found:
                for r in range(2):
                    slots[c, way, 2 * position(nz, d) + r] = choose(c, d, 0, dest, r)
            y_copy[c, way, t] = start(
                remote(
                    slots.at[c, way, pl.ds(low, 2 * len(found))],
                    pools[c].at[pl.ds(2 * nz * way + low, 2 * len(found))],
                    y_send.at[c, way, t],
                    y_recv.at[c, way, t],
                    at_y(dest),
                )
            )
        for d in found:
            for r in range(2):
                pools[c][6 * nz + 2 * position(nz, d) + r] = choose(c, d, 0, 0, r)
                if FAR[c]:
                    pools[c][4 * nz + 2 * position(nz, d) + r] = choose(c, d, 2, 0, r)

    def hand(c, unused):
        receive([copy for key, copy in y_copy.items() if key[0] == c])
        rows = pl.ds(pl.multiple_of(me * ROWS, ROWS), ROWS)
        for o in range(1, nm):
            j = lax.rem(me + o, nm)
            for k in range(count):
                parcels[c, o, k] = pools[c][places[j * count + k]]
            x_copy[c, o] = start(
                remote(
                    parcels.at[c, o],
                    sides.at[c, :, rows, :],
                    x_send.at[c, o],
                    x_recv.at[c, o],
                    column_peers[o - 1],
                )
            )
        for k in range(count):
            sides[c, k, rows, :] = pools[c][places[me * count + k]]

    acts = (near, send_slots, hand)
    asked = False
    for kind, c, t in ORDER:
        if not asked and kind == 1:
            asked = True
            receive(asking)
            to_scalars = pltpu.make_async_copy(w_near, w_held, local.at[6])
            to_scalars.start()
            to_scalars.wait()
        acts[kind](c, t)
    for load in loads[1:]:
        load.wait()
    finish(keep=nm - 1)
    for c in range(chunks):
        receive([x_copy[c, o] for o in range(1, nm)])
        project(c, sides, w_query, w_keyval, gains, query, keyval)

    @pl.loop(0, count)
    def one_side(i):
        attend(i, sides, w_out, w_head, gains, query, keyval, context, ordered, out)

    receive(
        [
            start(remote(out.at[lax.rem(me + o, nm)], block.at[me], s1.at[o], r1.at[o], column_peers[o - 1]))
            for o in range(1, nm)
        ]
    )
    block[me] = out[me]
    row = lax.broadcasted_iota(jnp.int32, (nv * 8, nm * 8), 0)
    toward[...] = jnp.dot(
        jnp.where(row == keys[0:1, 0 : nm * 8], 1.0, 0.0),
        block[...].reshape(nm * 8, 128),
        precision=lax.Precision.HIGHEST,
        preferred_element_type=jnp.float32,
    ).reshape(nv, 8, 128)
    came[z] = toward[pl.ds(z * NY, NY)]
    receive(
        [
            start(
                remote(
                    toward.at[pl.ds(lax.rem(z + o, nz) * NY, NY)], came.at[z], s2.at[o], r2.at[o], at_z(o)
                )
            )
            for o in range(1, nz)
        ]
    )
    half[...] = jnp.sum(came[...], axis=0)
    came_y[y] = half[y]
    receive(
        [
            start(remote(half.at[lax.rem(y + o, NY)], came_y.at[y], s4.at[o], r4.at[o], at_y(o)))
            for o in range(1, NY)
        ]
    )
    mine_sum[...] = jnp.sum(came_y[...], axis=0)
    every[me] = mine_sum[...]
    receive(
        [
            start(remote(mine_sum, every.at[me], s3.at[o], r3.at[o], column_peers[o - 1]))
            for o in range(1, nm)
        ]
    )
    blocks = tokv // 128
    for index in range(view_dev):
        for row in range(4 * blocks):
            place = row % blocks * 128
            sums[index, row // blocks, place : place + 128] = every[row // 2, index * 2 + row % 2]
    finish()


def on_device(tokens, pairs, w_embed, w_query, w_keyval, w_out, w_head, gains):
    nv = lax.axis_size("view")
    nm = lax.axis_size("mp")
    nz = nv // NY
    view_dev, tokv, feat = tokens.shape
    width = w_embed.shape[1]
    count = 2 * pairs.shape[0] // nm
    ask = (8, 128)
    part = tokv // nm
    chunks = part // ROWS
    piece = (ROWS, width)
    f32, bf16, i32 = jnp.float32, jnp.bfloat16, jnp.int32
    vmem = pl.BlockSpec(memory_space=pltpu.VMEM)
    hbm = pl.BlockSpec(memory_space=pltpu.HBM)
    dma = pltpu.SemaphoreType.DMA
    weights = (w_embed, w_query, w_keyval, w_out)
    return pl.pallas_call(
        functools.partial(kernel, nz, nm, chunks),
        out_shape=jax.ShapeDtypeStruct((view_dev, 4, tokv), f32),
        in_specs=[hbm, pl.BlockSpec(memory_space=pltpu.SMEM), vmem, vmem] + [hbm] * 4,
        out_specs=vmem,
        scratch_shapes=[pltpu.VMEM(w.shape, bf16) for w in weights]
        + [
            pltpu.VMEM(ask, i32),
            pltpu.VMEM(ask, i32),
            pltpu.SMEM((2 * pairs.shape[0],), i32),
            pltpu.VMEM((view_dev, part, nm * feat), bf16),
            pltpu.VMEM((NY,) + ask, i32),
            pltpu.SMEM((NY,) + ask, i32),
            pltpu.VMEM((chunks, 3, 2 * nz) + piece, bf16),
            pltpu.VMEM((chunks, nm, count) + piece, bf16),
            pltpu.VMEM((chunks, count, nm * ROWS, width), bf16),
            pltpu.VMEM((count, tokv, width), bf16),
            pltpu.VMEM((count, tokv, 2 * width), bf16),
            pltpu.VMEM((tokv, width), bf16),
            pltpu.VMEM((tokv, width), bf16),
            pltpu.VMEM((nm, 8, 128), f32),
            pltpu.VMEM((nm, 8, 128), f32),
            pltpu.VMEM((nv, 8, 128), f32),
            pltpu.VMEM((nz, NY, 8, 128), f32),
            pltpu.VMEM((NY, 8, 128), f32),
            pltpu.VMEM((NY, 8, 128), f32),
            pltpu.VMEM((8, 128), f32),
            pltpu.VMEM((nm, 8, 128), f32),
        ]
        + [pltpu.VMEM((8 * nz,) + piece, bf16)] * chunks
        + [
            pltpu.VMEM(((2 if FAR[c] else 1) * view_dev,) + piece, bf16)
            for c in range(chunks)
            for unused in range(nz)
        ]
        + [dma((7,))]
        + [dma((nm,))] * 2
        + [dma((nz,))] * 2
        + [dma((NY,))] * 2
        + [dma((nm,))] * 4
        + [dma((NY,))] * 2
        + [dma((chunks, nz))] * 2
        + [dma((chunks,))] * 2
        + [dma((chunks, 3, nz // 2 + 1))] * 2
        + [dma((chunks, nm))] * 2,
        compiler_params=pltpu.CompilerParams(
            collective_id=0, has_side_effects=True, vmem_limit_bytes=60 * 2**20
        ),
    )(tokens, pairs.T, w_head, jnp.transpose(gains, (1, 0, 2)), *weights)


def solution(mesh):
    return jax.shard_map(
        on_device,
        mesh=mesh,
        in_specs=(P("view", None, "mp"), P("view", None), P(), P(), P(), P(), P(), P()),
        out_specs=P("view", None, None),
        check_vma=False,
    )
```

```python
import functools

import jax
import jax.numpy as jnp
from jax import lax
from jax.experimental import pallas as pl
from jax.experimental.pallas import tpu as pltpu
from jax.sharding import PartitionSpec as P

HEADS = 12
NY = 4
ROWS = 16
MESH = pl.DeviceIdType.MESH
FAR = (False, False, True)
ORDER = (
    (0, 0, 0),
    (0, 1, 0),
    (1, 0, 0),
    (0, 0, 1),
    (1, 0, 1),
    (0, 1, 1),
    (1, 1, 1),
    (0, 0, 2),
    (0, 1, 2),
    (0, 0, 3),
    (0, 2, 0),
    (1, 0, 2),
    (1, 0, 3),
    (0, 1, 3),
    (0, 2, 1),
    (0, 0, 4),
    (1, 0, 4),
    (1, 1, 0),
    (1, 1, 2),
    (0, 1, 4),
    (0, 2, 2),
    (2, 0, 0),
    (1, 1, 4),
    (1, 1, 3),
    (0, 2, 3),
    (1, 2, 2),
    (1, 2, 3),
    (0, 2, 4),
    (1, 2, 4),
    (2, 1, 0),
    (1, 2, 1),
    (1, 2, 0),
    (2, 2, 0),
)


def normal(values):
    mean = jnp.mean(values, axis=-1, keepdims=True)
    centred = values - mean
    var = jnp.mean(centred * centred, axis=-1, keepdims=True)
    return centred * lax.rsqrt(var + 1e-06)


def remote(source, target, send, arrive, device):
    return pltpu.make_async_remote_copy(
        src_ref=source,
        dst_ref=target,
        send_sem=send,
        recv_sem=arrive,
        device_id=device,
        device_id_type=MESH,
    )


def offsets(nz, c, t):
    up = nz // 2 if c % 2 == 0 else (nz - 1) // 2
    down = nz - 1 - up
    if t == 0:
        return [(0, (1,) * (up > 0) + (-1,) * (down > 0))]
    found = []
    if t <= up:
        found.append((nz - t, (1,) * (t < up)))
    if t <= down:
        found.append((t, (-1,) * (t < down)))
    return found


def position(nz, d):
    return 0 if d == 0 else 2 * d if d < nz - d else 2 * (nz - d) - 1


def project(c, sides, w_query, w_keyval, gains, query, keyval):
    chunks, count, rows, width = sides.shape
    f32, bf16 = jnp.float32, jnp.bfloat16
    pairs = count // 2
    for side in range(2):
        views = jnp.concatenate([sides[c, 2 * p + side] for p in range(pairs)], axis=0)
        level = normal(views.astype(f32))
        query_in = (level * gains[0, side : side + 1]).astype(bf16)
        found = jnp.dot(query_in, w_query[side], preferred_element_type=f32).astype(bf16)
        for p in range(pairs):
            query[2 * p + side, c * rows : (c + 1) * rows] = found[p * rows : (p + 1) * rows]
        memory_in = (level * gains[1, 1 - side : 2 - side]).astype(bf16)
        found = jnp.dot(memory_in, w_keyval[1 - side], preferred_element_type=f32).astype(bf16)
        for p in range(pairs):
            keyval[2 * p + 1 - side, c * rows : (c + 1) * rows] = found[p * rows : (p + 1) * rows]


def attend(i, sides, w_out, w_head, gains, query, keyval, context, ordered, out):
    chunks, count, rows, width = sides.shape
    tokv = chunks * rows
    size = width // HEADS
    scale = 1.4426950408889634 / size**0.5
    f32, bf16 = jnp.float32, jnp.bfloat16
    side = lax.rem(i, 2)
    lane = lax.broadcasted_iota(jnp.int32, (tokv, 2 * size), 1)
    first = lane < size
    zero = jnp.zeros((tokv, 2 * size), bf16)
    ones = jnp.ones((tokv, 2 * size), bf16)
    counts = jnp.concatenate([jnp.where(first, ones, zero), jnp.where(first, zero, ones)], axis=0)

    def stack(columns):
        both = keyval[i, :, columns]
        return jnp.concatenate([jnp.where(first, both, zero), jnp.where(first, zero, both)], axis=0)

    def score(h):
        columns = slice(h * size, (h + 2) * size)
        return lax.dot_general(
            query[i, :, columns], stack(columns), (((1,), (1,)), ((), ())), preferred_element_type=f32
        )

    ahead = score(0)
    for h in range(0, HEADS, 2):
        scores = ahead
        if h + 2 < HEADS:
            ahead = score(h + 2)
        probs = []
        for half in range(2):
            own = scores[:, half * tokv : (half + 1) * tokv]
            top = jnp.max(own, axis=-1, keepdims=True)
            probs.append(jnp.exp2((own - top) * scale).astype(bf16))
        values = stack(slice(width + h * size, width + (h + 2) * size))
        total = jnp.dot(
            jnp.concatenate(probs, axis=1),
            jnp.concatenate([values, counts], axis=1),
            preferred_element_type=f32,
        )
        context[:, h * size : (h + 2) * size] = (total[:, : 2 * size] / total[:, 2 * size :]).astype(bf16)
    emb = jnp.concatenate([sides[c, i] for c in range(chunks)], axis=0)
    updated = emb.astype(f32) + jnp.dot(context[...], w_out[side], preferred_element_type=f32)
    final = (normal(updated) * gains[2, pl.ds(side, 1)]).astype(bf16)
    parts = rows // ROWS
    for c in range(chunks):
        for j in range(parts):
            place = (j * chunks + c) * ROWS
            come = (c * parts + j) * ROWS
            ordered[place : place + ROWS] = final[come : come + ROWS]
    head = lax.dot_general(
        w_head[side], ordered[...], (((1,), (1,)), ((), ())), preferred_element_type=f32
    )
    conf = 1.0 + jnp.exp(head[3:4])
    for c in range(4):
        record = conf * head[c : c + 1] if c < 3 else conf
        for b in range(tokv // 128):
            row = c * (tokv // 128) + b
            out[row // 2, pl.ds(row % 2 * count + i, 1), :] = record[:, b * 128 : (b + 1) * 128]


def plan(nz, count, view_dev, z, y, pairs, wanted, keys, places):
    total = 2 * pairs.shape[1]
    shape = wanted.shape
    lane = lax.broadcasted_iota(jnp.int32, shape, 1)
    views = [pairs[k % 2, k // 2] for k in range(total)]
    bits = view_dev.bit_length() - 1
    owners = [lax.shift_right_logical(v, bits) for v in views]
    asks = jnp.zeros(shape, jnp.int32)
    labels = jnp.zeros(shape, jnp.int32)
    for k in range(total):
        rank = jnp.int32(0)
        for j in range(k):
            rank = jnp.where(owners[j] == owners[k], 1, rank)
        asks = jnp.where(lane == owners[k] * 2 + rank, views[k] & (view_dev - 1), asks)
        for sub in range(2):
            spot = k // count * 2 * count + sub * count + k % count
            labels = jnp.where(lane == spot, views[k] * 2 + sub, labels)
        d = (lax.shift_right_logical(owners[k], NY.bit_length() - 1) - z + nz) & (nz - 1)
        come = (owners[k] - y + NY) & (NY - 1)
        base = jnp.where(come == 0, 3, jnp.where(come == NY - 1, 0, come))
        spot = jnp.where(d == 0, 0, jnp.where(2 * d < nz, 2 * d, 2 * (nz - d) - 1))
        places[k] = base * (2 * nz) + 2 * spot + rank
    wanted[...] = asks
    keys[...] = labels


def kernel(nz, nm, chunks, *refs):
    refs = iter(refs)

    def take(n):
        return [next(refs) for unused in range(n)]

    tokens, pairs, w_head, gains = take(4)
    in_hbm = take(4)
    (sums,) = take(1)
    w_embed, w_query, w_keyval, w_out = in_vmem = take(4)
    wanted, keys, places, full, w_near, w_held, slots, parcels, sides = take(9)
    query, keyval, context, ordered, out, block, toward, came, half, came_y, mine_sum, every = take(12)
    pools = take(chunks)
    held = [take(nz) for unused in range(chunks)]
    (local, s1, r1, s2, r2, s4, r4, s3, r3, t_send, t_recv, w_send, w_recv) = take(13)
    (z_send, z_recv, p_send, p_recv, y_send, y_recv, x_send, x_recv) = take(8)

    view = lax.axis_index("view")
    me = lax.axis_index("mp")
    z = view // NY
    y = view % NY
    nv = nz * NY
    part = tokens.shape[1] // nm
    feat = tokens.shape[2]
    view_dev = tokens.shape[0]
    total = 2 * pairs.shape[1]
    count = total // nm
    tokv = tokens.shape[1]

    def at_z(step):
        return (lax.rem(z + step + nz, nz) * NY + y, me)

    def at_y(step):
        return (z * NY + lax.rem(y + step + NY, NY), me)

    column_peers = [(view, lax.rem(me + o, nm)) for o in range(1, nm)]
    peers = column_peers + [at_z(o) for o in range(1, nz)] + [at_y(o) for o in range(1, NY)]
    barrier = pltpu.get_barrier_semaphore()
    for peer in peers:
        pl.semaphore_signal(barrier, inc=1, device_id=peer, device_id_type=MESH)
    loads = [pltpu.make_async_copy(a, b, local.at[k]) for k, (a, b) in enumerate(zip(in_hbm, in_vmem))]
    loads[0].start()
    own = pltpu.make_async_copy(
        tokens.at[:, pl.ds(pl.multiple_of(me * part, ROWS), part), :],
        full.at[:, :, pl.ds(pl.multiple_of(me * feat, 128), feat)],
        local.at[4],
    )
    own.start()
    plan(nz, count, view_dev, z, y, pairs, wanted, keys, places)
    w_near[0] = wanted[...]
    pl.semaphore_wait(barrier, len(peers))

    sent = []

    def start(copy):
        copy.start()
        sent.append(copy)
        return copy

    def finish(keep=0):
        for copy in sent[: len(sent) - keep]:
            copy.wait_send()
        del sent[: len(sent) - keep]

    def receive(copies):
        for copy in copies:
            copy.wait_recv()

    arriving = []
    for o in range(1, nm):
        j = lax.rem(me + o, nm)
        arriving.append(
            start(
                remote(
                    tokens.at[:, pl.ds(pl.multiple_of(j * part, ROWS), part), :],
                    full.at[:, :, pl.ds(pl.multiple_of(me * feat, 128), feat)],
                    t_send.at[o],
                    t_recv.at[o],
                    column_peers[o - 1],
                )
            )
        )
    asking = [
        start(remote(wanted, w_near.at[NY - o], w_send.at[o], w_recv.at[NY - o], at_y(o)))
        for o in range(1, NY)
    ]
    own.wait()
    loads[0].wait()
    receive(arriving)
    emb = jnp.dot(
        full[...].reshape(view_dev * part, nm * feat), w_embed[...], preferred_element_type=jnp.float32
    )
    emb = emb.astype(jnp.bfloat16).reshape(view_dev, part, -1)
    for c in range(chunks):
        held[c][0][0:view_dev] = emb[:, c * ROWS : (c + 1) * ROWS]

    z_copy, y_copy, x_copy = {}, {}, {}
    p_copy = {
        c: start(
            remote(
                held[c][0].at[pl.ds(0, view_dev)],
                held[c][0].at[pl.ds(view_dev, view_dev)],
                p_send.at[c],
                p_recv.at[c],
                at_y(2),
            )
        )
        for c in range(chunks)
        if FAR[c]
    }
    first_slot = [lax.rem(z + d, nz) * (NY * 2) for d in range(nz)]
    column_slot = [lax.rem(y + dy, NY) * 2 for dy in range(NY)]

    def choose(c, d, column, dest, r):
        local = w_held[dest, 0, first_slot[d] + column_slot[column] + r]
        return held[c][d][local if column == 0 else local + view_dev]

    def near(c, t):
        if t == 0 and FAR[c]:
            p_copy[c].wait_recv()
        for d, ways in offsets(nz, c, t):
            if t:
                z_copy[c, d].wait_recv()
            for way in ways:
                target = (d - way) % nz
                z_copy[c, target] = start(
                    remote(
                        held[c][d],
                        held[c][target],
                        z_send.at[c, target],
                        z_recv.at[c, target],
                        at_z(way),
                    )
                )

    def send_slots(c, t):
        found = [d for d, unused in offsets(nz, c, t)]
        low = 2 * min(position(nz, d) for d in found)
        for way, dest in enumerate((1, 3) if FAR[c] else (1, 3, 2)):
            for d in found:
                for r in range(2):
                    slots[c, way, 2 * position(nz, d) + r] = choose(c, d, 0, dest, r)
            y_copy[c, way, t] = start(
                remote(
                    slots.at[c, way, pl.ds(low, 2 * len(found))],
                    pools[c].at[pl.ds(2 * nz * way + low, 2 * len(found))],
                    y_send.at[c, way, t],
                    y_recv.at[c, way, t],
                    at_y(dest),
                )
            )
        for d in found:
            for r in range(2):
                pools[c][6 * nz + 2 * position(nz, d) + r] = choose(c, d, 0, 0, r)
                if FAR[c]:
                    pools[c][4 * nz + 2 * position(nz, d) + r] = choose(c, d, 2, 0, r)

    def hand(c, unused):
        receive([copy for key, copy in y_copy.items() if key[0] == c])
        rows = pl.ds(pl.multiple_of(me * ROWS, ROWS), ROWS)
        for o in range(1, nm):
            j = lax.rem(me + o, nm)
            for k in range(count):
                parcels[c, o, k] = pools[c][places[j * count + k]]
            x_copy[c, o] = start(
                remote(
                    parcels.at[c, o],
                    sides.at[c, :, rows, :],
                    x_send.at[c, o],
                    x_recv.at[c, o],
                    column_peers[o - 1],
                )
            )
        for k in range(count):
            sides[c, k, rows, :] = pools[c][places[me * count + k]]

    acts = (near, send_slots, hand)
    asked = False
    for kind, c, t in ORDER:
        if not asked and kind == 1:
            asked = True
            receive(asking)
            to_scalars = pltpu.make_async_copy(w_near, w_held, local.at[6])
            to_scalars.start()
            to_scalars.wait()
            for load in loads[1:]:
                load.start()
        acts[kind](c, t)
    for load in loads[1:]:
        load.wait()
    finish(keep=nm - 1)
    for c in range(chunks):
        receive([x_copy[c, o] for o in range(1, nm)])
        project(c, sides, w_query, w_keyval, gains, query, keyval)

    @pl.loop(0, count)
    def one_side(i):
        attend(i, sides, w_out, w_head, gains, query, keyval, context, ordered, out)

    receive(
        [
            start(remote(out.at[lax.rem(me + o, nm)], block.at[me], s1.at[o], r1.at[o], column_peers[o - 1]))
            for o in range(1, nm)
        ]
    )
    block[me] = out[me]
    row = lax.broadcasted_iota(jnp.int32, (nv * 8, nm * 8), 0)
    toward[...] = jnp.dot(
        jnp.where(row == keys[0:1, 0 : nm * 8], 1.0, 0.0),
        block[...].reshape(nm * 8, 128),
        precision=lax.Precision.HIGHEST,
        preferred_element_type=jnp.float32,
    ).reshape(nv, 8, 128)
    came[z] = toward[pl.ds(z * NY, NY)]
    receive(
        [
            start(
                remote(
                    toward.at[pl.ds(lax.rem(z + o, nz) * NY, NY)], came.at[z], s2.at[o], r2.at[o], at_z(o)
                )
            )
            for o in range(1, nz)
        ]
    )
    half[...] = jnp.sum(came[...], axis=0)
    came_y[y] = half[y]
    receive(
        [
            start(remote(half.at[lax.rem(y + o, NY)], came_y.at[y], s4.at[o], r4.at[o], at_y(o)))
            for o in range(1, NY)
        ]
    )
    mine_sum[...] = jnp.sum(came_y[...], axis=0)
    every[me] = mine_sum[...]
    receive(
        [
            start(remote(mine_sum, every.at[me], s3.at[o], r3.at[o], column_peers[o - 1]))
            for o in range(1, nm)
        ]
    )
    blocks = tokv // 128
    for index in range(view_dev):
        for row in range(4 * blocks):
            place = row % blocks * 128
            sums[index, row // blocks, place : place + 128] = every[row // 2, index * 2 + row % 2]
    finish()


def on_device(tokens, pairs, w_embed, w_query, w_keyval, w_out, w_head, gains):
    nv = lax.axis_size("view")
    nm = lax.axis_size("mp")
    nz = nv // NY
    view_dev, tokv, feat = tokens.shape
    width = w_embed.shape[1]
    count = 2 * pairs.shape[0] // nm
    ask = (8, 128)
    part = tokv // nm
    chunks = part // ROWS
    piece = (ROWS, width)
    f32, bf16, i32 = jnp.float32, jnp.bfloat16, jnp.int32
    vmem = pl.BlockSpec(memory_space=pltpu.VMEM)
    hbm = pl.BlockSpec(memory_space=pltpu.HBM)
    dma = pltpu.SemaphoreType.DMA
    weights = (w_embed, w_query, w_keyval, w_out)
    return pl.pallas_call(
        functools.partial(kernel, nz, nm, chunks),
        out_shape=jax.ShapeDtypeStruct((view_dev, 4, tokv), f32),
        in_specs=[hbm, pl.BlockSpec(memory_space=pltpu.SMEM), vmem, vmem] + [hbm] * 4,
        out_specs=vmem,
        scratch_shapes=[pltpu.VMEM(w.shape, bf16) for w in weights]
        + [
            pltpu.VMEM(ask, i32),
            pltpu.VMEM(ask, i32),
            pltpu.SMEM((2 * pairs.shape[0],), i32),
            pltpu.VMEM((view_dev, part, nm * feat), bf16),
            pltpu.VMEM((NY,) + ask, i32),
            pltpu.SMEM((NY,) + ask, i32),
            pltpu.VMEM((chunks, 3, 2 * nz) + piece, bf16),
            pltpu.VMEM((chunks, nm, count) + piece, bf16),
            pltpu.VMEM((chunks, count, nm * ROWS, width), bf16),
            pltpu.VMEM((count, tokv, width), bf16),
            pltpu.VMEM((count, tokv, 2 * width), bf16),
            pltpu.VMEM((tokv, width), bf16),
            pltpu.VMEM((tokv, width), bf16),
            pltpu.VMEM((nm, 8, 128), f32),
            pltpu.VMEM((nm, 8, 128), f32),
            pltpu.VMEM((nv, 8, 128), f32),
            pltpu.VMEM((nz, NY, 8, 128), f32),
            pltpu.VMEM((NY, 8, 128), f32),
            pltpu.VMEM((NY, 8, 128), f32),
            pltpu.VMEM((8, 128), f32),
            pltpu.VMEM((nm, 8, 128), f32),
        ]
        + [pltpu.VMEM((8 * nz,) + piece, bf16)] * chunks
        + [
            pltpu.VMEM(((2 if FAR[c] else 1) * view_dev,) + piece, bf16)
            for c in range(chunks)
            for unused in range(nz)
        ]
        + [dma((7,))]
        + [dma((nm,))] * 2
        + [dma((nz,))] * 2
        + [dma((NY,))] * 2
        + [dma((nm,))] * 4
        + [dma((NY,))] * 2
        + [dma((chunks, nz))] * 2
        + [dma((chunks,))] * 2
        + [dma((chunks, 3, nz // 2 + 1))] * 2
        + [dma((chunks, nm))] * 2,
        compiler_params=pltpu.CompilerParams(
            collective_id=0, has_side_effects=True, vmem_limit_bytes=60 * 2**20
        ),
    )(tokens, pairs.T, w_head, jnp.transpose(gains, (1, 0, 2)), *weights)


def solution(mesh):
    return jax.shard_map(
        on_device,
        mesh=mesh,
        in_specs=(P("view", None, "mp"), P("view", None), P(), P(), P(), P(), P(), P()),
        out_specs=P("view", None, None),
        check_vma=False,
    )
```
